32 devices in a mesh: groups: 2 (over y), row: 4 (over z), col: 4 (over x, core).
Axes of the slice: x: 2, y: 2, z: 4, core: 2. Of those that a mesh axis runs over, the one named last changes fastest.
Arguments:
- embeddings: bfloat16 [8192, 256], P(('groups', 'row', 'col')), parts along dimension 0, may hold values from -6 to 6
- tile_list: int32 [8, 4, 2, 48], P(('groups', 'row'), 'col'), parts along dimension 0, may hold values from 0 to 7, as said below
- tile_count: int32 [8, 4], P(('groups', 'row'), 'col'), parts along dimension 0, may hold values from 8 to 48, as said below
- seeds: int32 [128, 128], P('groups'), parts along dimension 0, may hold values from 0 to 4095
Outputs:
- ranks: float32 [8192, 64], P(('groups', 'row', 'col')), parts along dimension 0
The draws below stay inside these ranges and needn't reach their ends.
There are 2 independent parts, one for each index of `groups`. The reference program is written for one: setup_inputs(seed, part) draws one part's arguments, and reference() takes and returns one part's arrays. A program takes and returns all parts, laid end to end along the dimension named above; each array names one. Nothing has to cross between parts.
Inputs may be any that keep to these rules, and one draw needn't show every extreme that they name: `tile_list`: row tile entries are below 8, column tile entries below 8; within a cell the 48 slots name distinct pairs, and slot p names row tile p for p < 8. `tile_count`: some cell in every draw has all 48 slots live.
All inputs are finite; a program needn't handle non-finite values.
Results may differ from the reference program's by a relative error of at most 0.006.
Values may be sent and summed in bfloat16 or wider, within the bound.
No kernel may reach another device: no remote copies, remote signals or barrier semaphores. Data moves between devices by JAX's collectives and lax.ppermute only.
A program may use at most 64 MiB of HBM per device.

```python
import jax
import jax.numpy as jnp
from jax import lax

EMBED = 256
SEED_COLS = 64
TILE = 128
ROW_TILES = 8
ITERS = 3
SEED_SHARE = 32
COL_TILES = 8
SLOTS = 48
SESS = 4096
SEEDS = 128
N_ROW = 4
N_COL = 4


def tile_plan(key):
    plan_key = jax.random.fold_in(key, 11)
    score_key, forced_key, level_key, busiest_key = jax.random.split(plan_key, 4)
    cell_count = N_ROW * N_COL
    grid_slots = ROW_TILES * COL_TILES
    ceiling = max(2, 2 ** 30 // grid_slots - 1)
    scores = jax.random.randint(score_key, (cell_count, grid_slots), 1, ceiling, dtype=jnp.int32)
    forced = jax.random.randint(forced_key, (cell_count, ROW_TILES), 0, COL_TILES, dtype=jnp.int32)
    slot_ids = jnp.arange(grid_slots, dtype=jnp.int32)
    slot_rows = slot_ids // COL_TILES
    slot_cols = slot_ids % COL_TILES
    forced_cols = jnp.take(forced, slot_rows, axis=1)
    priority = jnp.where(slot_cols[None, :] == forced_cols, 0, scores) * grid_slots + slot_ids[None, :]
    chosen = jnp.argsort(priority, axis=1)[:, :SLOTS].astype(jnp.int32)
    listing = jnp.stack([chosen // COL_TILES, chosen % COL_TILES], axis=1).reshape(N_ROW, N_COL, 2, SLOTS)
    levels = jax.random.randint(level_key, (cell_count,), 1, 33, dtype=jnp.int32)
    busiest = jax.random.randint(busiest_key, (), 0, cell_count, dtype=jnp.int32)
    levels = jnp.where(jnp.arange(cell_count, dtype=jnp.int32) == busiest, 32, levels)
    counts = ROW_TILES + (SLOTS - ROW_TILES) * levels * levels // 1024
    return (listing.astype(jnp.int32), counts.reshape(N_ROW, N_COL).astype(jnp.int32))


def draw_tile_list(key, part):
    return tile_plan(key)[0]


def draw_tile_count(key, part):
    return tile_plan(key)[1]


def plant(drawn, stream_key, low, high):
    place = [jax.random.randint(jax.random.fold_in(stream_key, axis), (), 0, length) for axis, length in enumerate(drawn.shape)]
    longest = drawn.shape.index(max(drawn.shape))
    beside = place[:longest] + [(place[longest] + 1) % drawn.shape[longest]] + place[longest + 1:]
    return drawn.at[tuple(place)].set(low).at[tuple(beside)].set(high)


def block_scale(own_key, shape, shards, least, largest):
    gain, own = 1.0, jax.random.fold_in(own_key, 6)
    for position, parts in shards:
        draws = jnp.exp(jax.random.uniform(jax.random.fold_in(own, position), (parts,), jnp.float32, least / len(shards), largest / len(shards)))
        gain = gain * jnp.repeat(draws, shape[position] // parts).reshape([-1 if axis == position else 1 for axis in range(len(shape))])
    return gain


def gaussian(key, shape, width, reach, cuts=(), held_as=jnp.bfloat16):
    values = width * jax.random.normal(key, shape, jnp.float32)
    if cuts:
        values = values * block_scale(key, shape, cuts, -0.22, 0.18)
    return jnp.clip(values, -reach, reach).astype(held_as)


def setup_inputs(seed: int = 0, part: int = 0) -> dict:
    key_list = jax.random.split(jax.random.key(seed), 5)
    own_keys = jax.random.split(jax.random.fold_in(key_list[4], part), 5)
    embeddings = gaussian(own_keys[0], (SESS, EMBED), 1.0, 6.0, ((0, 16),))
    tile_list = draw_tile_list(jax.random.fold_in(jax.random.fold_in(key_list[4], part), 71), part)
    tile_count = draw_tile_count(jax.random.fold_in(jax.random.fold_in(key_list[4], part), 71), part)
    seeds = plant(jax.random.randint(own_keys[3], (SEED_COLS, SEEDS), 0, SESS), jax.random.fold_in(own_keys[3], 1), 0, SESS - 1).astype(jnp.int32)
    return dict(embeddings=embeddings, tile_list=tile_list, tile_count=tile_count, seeds=seeds)


KERNEL_GAIN = 4.0
DAMPING = 0.85
EPSILON = 1e-06

def normalize(rows_in):
    widened = rows_in.astype(jnp.float32)
    factor = lax.rsqrt(lax.optimization_barrier(jnp.mean(widened * widened, axis=-1, keepdims=True)) + EPSILON)
    return (widened * factor * widened.shape[-1] ** (-0.5)).astype(jnp.bfloat16)

def reference(embeddings, tile_list, tile_count, seeds):
    unit_rows = normalize(embeddings)
    grid_rows = ROW_TILES * TILE
    slice_rows = grid_rows // N_COL
    positions = jnp.arange(COL_TILES * TILE, dtype=jnp.int32)
    cell_ids = jnp.arange(N_ROW * N_COL, dtype=jnp.int32)
    tile_lists = tile_list.reshape(N_ROW * N_COL, 2, SLOTS)
    counts = tile_count.reshape(N_ROW * N_COL)
    slot_ids = jnp.arange(SLOTS, dtype=jnp.int32)

    def column_sessions(col_pos):
        return (positions // slice_rows * grid_rows + col_pos * slice_rows + positions % slice_rows).astype(jnp.int32)

    def kernel_cell(cell_id):
        row_pos = cell_id // N_COL
        col_pos = cell_id % N_COL
        row_emb = lax.dynamic_slice_in_dim(unit_rows, (row_pos * grid_rows).astype(jnp.int32), grid_rows, 0)
        row_emb = row_emb.reshape(ROW_TILES, TILE, EMBED)
        col_emb = jnp.take(unit_rows, column_sessions(col_pos), axis=0).reshape(COL_TILES, TILE, EMBED)
        row_ids = tile_lists[cell_id, 0]
        col_ids = tile_lists[cell_id, 1]
        live_mask = (slot_ids < counts[cell_id]).astype(jnp.float32)
        left_tiles = jnp.take(row_emb, row_ids, axis=0).astype(jnp.float32)
        right_tiles = jnp.take(col_emb, col_ids, axis=0).astype(jnp.float32)
        inner_prod = jnp.einsum('bie,bje->bij', left_tiles, right_tiles)
        values = jnp.exp(KERNEL_GAIN * (2.0 * inner_prod - 2.0)).astype(jnp.bfloat16)
        row_total = lax.optimization_barrier(jnp.sum(values.astype(jnp.float32), axis=2)) * live_mask[:, None]
        degree = jnp.zeros((ROW_TILES, TILE), jnp.float32).at[row_ids].add(row_total)
        return (values, degree)
    kernel, degree_cells = lax.map(kernel_cell, cell_ids)
    degree = lax.optimization_barrier(jnp.sum(degree_cells.reshape(N_ROW, N_COL, grid_rows), axis=1)).reshape(SESS)
    seed_columns = jnp.broadcast_to(jnp.arange(SEED_COLS, dtype=jnp.int32)[:, None], seeds.shape)
    restart = jnp.zeros((SESS, SEED_COLS), jnp.float32).at[seeds, seed_columns].add(float(SEED_SHARE))
    rank_rows = restart
    for sweep_idx in range(ITERS):
        rounded = rank_rows.astype(jnp.bfloat16)

        def apply_cell(pieces):
            cell_id, values = pieces
            col_pos = cell_id % N_COL
            col_ranks = jnp.take(rounded, column_sessions(col_pos), axis=0).reshape(COL_TILES, TILE, SEED_COLS)
            right_tiles = jnp.take(col_ranks, tile_lists[cell_id, 1], axis=0).astype(jnp.float32)
            product = jnp.einsum('bij,bjk->bik', values.astype(jnp.float32), right_tiles)
            live_mask = (slot_ids < counts[cell_id]).astype(jnp.float32)
            return jnp.zeros((ROW_TILES, TILE, SEED_COLS), jnp.float32).at[tile_lists[cell_id, 0]].add(product * live_mask[:, None, None])
        cell_terms = lax.map(apply_cell, (cell_ids, kernel))
        spread = lax.optimization_barrier(jnp.sum(cell_terms.reshape(N_ROW, N_COL, grid_rows, SEED_COLS), axis=1)).reshape(SESS, SEED_COLS)
        rank_rows = (1.0 - DAMPING) * restart + DAMPING * spread / degree[:, None]
    return rank_rows
```

```python
import functools
import math

import jax
import jax.numpy as jnp
from jax import lax
from jax.experimental import pallas as pl
from jax.experimental.pallas import tpu as pltpu
from jax.sharding import PartitionSpec as P

TILE = 128
ITERS = 3
SEED_SHARE = 32


KERNEL_GAIN = 4.0
DAMPING = 0.85
EPSILON = 1e-06

SLOPE = 2.0 * KERNEL_GAIN * math.log2(math.e)
DEAD = -1e9
MASK_ROWS = 16
EXTRA_ROWS = 16

F32 = jnp.float32
BF16 = jnp.bfloat16


def normalize(rows_in):
    widened = rows_in.astype(F32)
    factor = lax.rsqrt(jnp.mean(widened * widened, axis=-1, keepdims=True) + EPSILON)
    return (widened * factor * widened.shape[-1] ** (-0.5)).astype(BF16)


def dot_nt(lhs, rhs):
    return lax.dot_general(lhs, rhs, (((1,), (1,)), ((), ())), preferred_element_type=F32)


def dot_nn(lhs, rhs):
    return lax.dot_general(lhs, rhs, (((1,), (0,)), ((), ())), preferred_element_type=F32)


def payload_kernel(count_ref, emb_ref, list_ref, out_ref):
    rows = emb_ref.shape[0]
    width = emb_ref.shape[1]
    slots = list_ref.shape[1]
    out_ref[0:rows, :] = normalize(emb_ref[...])
    live = lax.broadcasted_iota(jnp.int32, (1, slots), 1) < count_ref[0, 0]
    col_hot = (lax.broadcasted_iota(jnp.int32, (EXTRA_ROWS, slots), 0) == list_ref[1:2, :]) & live
    row_hot = lax.broadcasted_iota(jnp.int32, (width, slots), 0) == list_ref[0:1, :]
    table = dot_nt(col_hot.astype(F32).astype(BF16), row_hot.astype(F32).astype(BF16))
    out_ref[rows : rows + EXTRA_ROWS, :] = table.astype(BF16)


def restart_kernel(me_ref, seeds_ref, out_ref, counts):
    seed_cols = seeds_ref.shape[0]
    tiles = counts.shape[1]
    me = me_ref[0]
    spot = lax.broadcasted_iota(jnp.int32, (tiles, TILE), 0)
    kk, xs, zs, half = spot // 16, (spot // 8) % 2, (spot // 2) % 4, spot % 2
    tile_ids = (me ^ (zs * 4 + xs * 2 + kk)) * 2 + half
    lows = lax.broadcasted_iota(jnp.int32, (TILE, TILE), 0)

    @pl.loop(0, seed_cols, unroll=4)
    def _(k):
        row = seeds_ref[pl.ds(k, 1), :]
        high_hot = (tile_ids == row // TILE).astype(F32).astype(BF16)
        low_hot = (lows == row % TILE).astype(F32).astype(BF16)
        counts[k] = dot_nt(high_hot, low_hot) * float(SEED_SHARE)

    for t in range(tiles):
        out_ref[0:seed_cols, t * TILE : (t + 1) * TILE] = counts[:, t, :].astype(BF16)
    rest = out_ref.shape[0] - seed_cols
    first = lax.broadcasted_iota(jnp.int32, (rest, out_ref.shape[1]), 0) == 0
    out_ref[seed_cols:, :] = first.astype(F32).astype(BF16)


def build_kernel(me_ref, rt_ref, *refs):
    blocks = refs[:16]
    kt_ref, next_ref, gain_ref, units, masks, bias, sems = refs[16:]
    me = me_ref[0]
    core, x_pos, z_pos = me % 2, (me // 2) % 2, me // 4
    rows = units.shape[0] // 16
    copies = []
    for s in range(16):
        copies.append(
            (
                pltpu.make_async_copy(
                    blocks[s].at[pl.ds(0, rows)], units.at[pl.ds(s * rows, rows)], sems.at[2 * s]
                ),
                pltpu.make_async_copy(
                    blocks[s].at[pl.ds(rows, EXTRA_ROWS)],
                    masks.at[pl.ds(s * EXTRA_ROWS, EXTRA_ROWS)],
                    sems.at[2 * s + 1],
                ),
            )
        )
    for one, two in copies:
        two.start()
    for one, two in copies:
        one.start()
    for one, two in copies:
        two.wait()
    width = masks.shape[1]
    pick_row = lax.broadcasted_iota(jnp.int32, (width, 512), 0)
    pick_col = lax.broadcasted_iota(jnp.int32, (width, 512), 1) // TILE
    wanted = 4 * (x_pos ^ (pick_col // 2)) + 2 * core + pick_col % 2
    pick = (pick_row == wanted).astype(F32).astype(BF16)
    spread_mask = dot_nn(masks[...], pick)
    spread_bias = jnp.where(spread_mask > 0.5, -SLOPE, DEAD)
    for group in range(4):
        for zs in range(4):
            cell = group * 4 + zs
            for xs in range(2):
                lane = (xs * 4 + zs) * rows
                bias[group * 8 : group * 8 + 8, lane : lane + rows] = spread_bias[
                    cell * EXTRA_ROWS : cell * EXTRA_ROWS + 8, xs * rows : (xs + 1) * rows
                ]
    for one, two in copies:
        one.wait()
    own = 8 * rows
    chunk = 512

    @pl.loop(0, 16)
    def _(s):
        group, zs = s // 4, s % 4
        start = pl.multiple_of(s * rows, rows)
        source = units[pl.ds(start, rows), :]
        bias_row = group * 8 + 2 * (z_pos ^ zs)
        for c in range(own // chunk):
            lanes = slice(c * chunk, (c + 1) * chunk)
            inner = dot_nt(source, units[lanes, :])
            for half in range(rows // TILE):
                shift = bias[pl.ds(bias_row + half, 1), lanes]
                value = jnp.exp2(inner[half * TILE : (half + 1) * TILE] * SLOPE + shift)
                kt_ref[pl.ds(pl.multiple_of(start + half * TILE, TILE), TILE), lanes] = value.astype(BF16)

    seed_cols = next_ref.shape[0]
    for c in range(own // chunk):
        lanes = slice(c * chunk, (c + 1) * chunk)
        total = dot_nn(rt_ref[...], kt_ref[:, lanes])
        gain = DAMPING / total[seed_cols : seed_cols + 8]
        gain_ref[:, lanes] = gain
        next_ref[:, lanes] = (
            (1.0 - DAMPING) * rt_ref[0:seed_cols, lanes].astype(F32) + total[0:seed_cols] * gain[0:1]
        ).astype(BF16)


def step_kernel(rt_ref, kt_ref, gain_ref, mine_ref, other_ref, out_ref):
    seed_cols = out_ref.shape[0]
    own = out_ref.shape[1]
    chunk = 512
    for c in range(own // chunk):
        lanes = slice(c * chunk, (c + 1) * chunk)
        total = dot_nn(mine_ref[...], kt_ref[0:own, lanes]) + dot_nn(other_ref[...], kt_ref[own:, lanes])
        out_ref[:, lanes] = (
            (1.0 - DAMPING) * rt_ref[0:seed_cols, lanes].astype(F32) + total * gain_ref[0:1, lanes]
        ).astype(BF16)


def last_kernel(rt_ref, kt_ref, gain_ref, mine_ref, other_ref, out_ref):
    seed_cols = out_ref.shape[1]
    rows = out_ref.shape[0]
    own = mine_ref.shape[1]
    total = dot_nn(mine_ref[...], kt_ref[0:own, 0:rows]) + dot_nn(other_ref[...], kt_ref[own:, 0:rows])
    ranks = (1.0 - DAMPING) * rt_ref[0:seed_cols, 0:rows].astype(F32) + total * gain_ref[0:1, 0:rows]
    out_ref[...] = ranks.T


WHOLE = pl.BlockSpec(memory_space=pltpu.VMEM)
SCALARS = pl.BlockSpec(memory_space=pltpu.SMEM)
REMAIN = pl.BlockSpec(memory_space=pl.ANY)


def params():
    return pltpu.CompilerParams(vmem_limit_bytes=20 * 2**20)


def swap(array, mapping):
    pairs = [(device, mapping(device)) for device in range(16)]
    return lax.ppermute(array, ("row", "col"), pairs)


def outer_pair(device):
    return device ^ 4


def inner_pair(device):
    z = device // 4
    return device ^ 12 if z in (1, 2) else device


def across(device):
    return device ^ 2


def sibling(device):
    return device ^ 1


def chip_local(embeddings, tile_list, tile_count, seeds):
    row_pos = lax.axis_index("row")
    me = (row_pos * 4 + lax.axis_index("col")).reshape(1)
    rows, width = embeddings.shape
    seed_cols = seeds.shape[0]
    sessions = rows * 16
    own = rows * 8
    slots = tile_list.shape[3]
    block = pl.pallas_call(
        payload_kernel,
        in_specs=[SCALARS, WHOLE, WHOLE],
        out_specs=WHOLE,
        out_shape=jax.ShapeDtypeStruct((rows + EXTRA_ROWS, width), BF16),
        compiler_params=params(),
        name="payload",
    )(tile_count, embeddings, tile_list.reshape(2, slots))

    is_end = (row_pos == 0) | (row_pos == 3)
    z1 = swap(block, outer_pair)
    near = swap(block, inner_pair)
    x0 = swap(block, across)
    far_a = swap(near, outer_pair)
    far_b = swap(z1, inner_pair)
    x1 = swap(z1, across)
    z2 = jnp.where(is_end, far_a, far_b)
    last = swap(far_b, outer_pair)
    x2 = swap(z2, across)
    z3 = jnp.where(is_end, last, near)
    x3 = swap(z3, across)
    mine = [block, z1, z2, z3, x0, x1, x2, x3]
    other = [swap(one, sibling) for one in mine]

    rt = pl.pallas_call(
        restart_kernel,
        in_specs=[SCALARS, WHOLE],
        out_specs=WHOLE,
        out_shape=jax.ShapeDtypeStruct((seed_cols + 16, sessions), BF16),
        scratch_shapes=[pltpu.VMEM((seed_cols, sessions // TILE, TILE), F32)],
        compiler_params=params(),
        name="restart",
    )(me, seeds)

    kt, ranks, gain = pl.pallas_call(
        build_kernel,
        in_specs=[SCALARS, WHOLE] + [REMAIN] * 16,
        out_specs=[WHOLE] * 3,
        out_shape=[
            pltpu.VMEM((sessions, own), BF16),
            jax.ShapeDtypeStruct((seed_cols, own), BF16),
            jax.ShapeDtypeStruct((8, own), F32),
        ],
        scratch_shapes=[
            pltpu.VMEM((sessions, width), BF16),
            pltpu.VMEM((16 * EXTRA_ROWS, width), BF16),
            pltpu.VMEM((32, own), F32),
            pltpu.SemaphoreType.DMA((32,)),
        ],
        compiler_params=params(),
        name="build",
    )(me, rt, *mine, *other)
    for sweep in range(ITERS - 2):
        ranks = pl.pallas_call(
            step_kernel,
            in_specs=[WHOLE] * 5,
            out_specs=WHOLE,
            out_shape=jax.ShapeDtypeStruct((seed_cols, own), BF16),
            compiler_params=params(),
            name="step",
        )(rt, kt, gain, ranks, swap(ranks, sibling))
    return pl.pallas_call(
        last_kernel,
        in_specs=[WHOLE] * 5,
        out_specs=WHOLE,
        out_shape=jax.ShapeDtypeStruct((rows, seed_cols), F32),
        compiler_params=params(),
        name="last",
    )(rt, kt, gain, ranks, swap(ranks, sibling))


def block_width():
    for option_width in (16, 8, 4, 2):
        return option_width
    return 1


def seed_mass(seed_index, is_valid, length):
    spots = jnp.arange(length, dtype=jnp.int32)

    def one_column(pieces):
        index_row, valid_row = pieces
        hits = (index_row[:, None] == spots[None, :]) & valid_row[:, None]
        return jnp.sum(hits.astype(jnp.float32), axis=0) * float(SEED_SHARE)

    table = lax.map(one_column, (seed_index, is_valid))
    return table.T


def grid_local(embeddings, tile_list, tile_count, seeds):
    n_row = lax.axis_size("row")
    n_col = lax.axis_size("col")
    row_pos = lax.axis_index("row")
    col_pos = lax.axis_index("col")
    slice_rows = embeddings.shape[0]
    grid_rows = slice_rows * n_col
    row_tiles = grid_rows // TILE
    col_tiles = slice_rows * n_row // TILE
    seed_cols = seeds.shape[0]
    unit_rows = normalize(embeddings)
    row_emb = lax.all_gather(unit_rows, "col", axis=0, tiled=True).reshape(row_tiles, TILE, -1)
    col_emb = lax.all_gather(unit_rows, "row", axis=0, tiled=True).reshape(col_tiles, TILE, -1)
    slots = tile_list.shape[3]
    width_b = block_width()
    turn_count = slots // width_b
    row_ids = tile_list[0, 0, 0]
    col_ids = tile_list[0, 0, 1]
    live_mask = (jnp.arange(slots, dtype=jnp.int32) < tile_count[0, 0]).astype(jnp.float32)
    row_blocks = row_ids.reshape(turn_count, width_b)
    col_blocks = col_ids.reshape(turn_count, width_b)
    live_blocks = live_mask.reshape(turn_count, width_b)

    def kernel_turn(degree, pieces):
        row_part, col_part, live_part = pieces
        left_tiles = jnp.take(row_emb, row_part, axis=0)
        right_tiles = jnp.take(col_emb, col_part, axis=0)
        inner_prod = jnp.einsum(
            "bie,bje->bij", left_tiles, right_tiles, preferred_element_type=jnp.float32
        )
        values = jnp.exp(KERNEL_GAIN * (2.0 * inner_prod - 2.0)).astype(jnp.bfloat16)
        row_total = jnp.sum(values.astype(jnp.float32), axis=2)
        degree = degree.at[row_part].add(row_total * live_part[:, None])
        return (degree, values)

    degree_part, kernel = lax.scan(
        kernel_turn,
        jnp.zeros((row_tiles, TILE), jnp.float32),
        (row_blocks, col_blocks, live_blocks),
    )
    degree_part = degree_part.reshape(grid_rows)

    def spread(ranks_col):
        col_ranks = ranks_col.reshape(col_tiles, TILE, seed_cols)

        def rank_turn(running, pieces):
            row_part, col_part, live_part, values = pieces
            right_tiles = jnp.take(col_ranks, col_part, axis=0)
            product = jnp.einsum(
                "bij,bjk->bik", values, right_tiles, preferred_element_type=jnp.float32
            )
            running = running.at[row_part].add(product * live_part[:, None, None])
            return (running, None)

        running, unused = lax.scan(
            rank_turn,
            jnp.zeros((row_tiles, TILE, seed_cols), jnp.float32),
            (row_blocks, col_blocks, live_blocks, kernel),
        )
        return running.reshape(grid_rows, seed_cols)

    own_start = (row_pos * n_col + col_pos) * slice_rows
    own_index = seeds - own_start
    seed_own = seed_mass(own_index, (own_index >= 0) & (own_index < slice_rows), slice_rows)
    degree = lax.psum_scatter(degree_part, "col", scatter_dimension=0, tiled=True)
    opening = lax.all_gather(seed_own.astype(jnp.bfloat16), "row", axis=0, tiled=True)
    partial_rows = spread(opening)
    summed = lax.psum_scatter(partial_rows, "col", scatter_dimension=0, tiled=True)
    rank_rows = (1.0 - DAMPING) * seed_own + DAMPING * summed / degree[:, None]
    for sweep_idx in range(ITERS - 1):
        gathered = lax.all_gather(rank_rows.astype(jnp.bfloat16), "row", axis=0, tiled=True)
        partial_rows = spread(gathered)
        summed = lax.psum_scatter(partial_rows, "col", scatter_dimension=0, tiled=True)
        rank_rows = (1.0 - DAMPING) * seed_own + DAMPING * summed / degree[:, None]
    return rank_rows


def solution(mesh):
    n_row, n_col = mesh.shape["row"], mesh.shape["col"]

    def local(embeddings, tile_list, tile_count, seeds):
        small = n_row == 4 and n_col == 4 and embeddings.shape == (2 * TILE, 2 * TILE)
        if small and seeds.shape == (64, TILE):
            return chip_local(embeddings, tile_list, tile_count, seeds)
        return grid_local(embeddings, tile_list, tile_count, seeds)

    return jax.shard_map(
        local,
        mesh=mesh,
        in_specs=(
            P(("groups", "row", "col"), None),
            P(("groups", "row"), "col", None, None),
            P(("groups", "row"), "col"),
            P("groups", None),
        ),
        out_specs=P(("groups", "row", "col"), None),
        check_vma=False,
    )
```

```python
import functools
import math

import jax
import jax.numpy as jnp
from jax import lax
from jax.experimental import pallas as pl
from jax.experimental.pallas import tpu as pltpu
from jax.sharding import PartitionSpec as P

TILE = 128
ITERS = 3
SEED_SHARE = 32


KERNEL_GAIN = 4.0
DAMPING = 0.85
EPSILON = 1e-06

SLOPE = 2.0 * KERNEL_GAIN * math.log2(math.e)
DEAD = -1e9
MASK_ROWS = 16
EXTRA_ROWS = 16

F32 = jnp.float32
BF16 = jnp.bfloat16


def normalize(rows_in):
    widened = rows_in.astype(F32)
    factor = lax.rsqrt(jnp.mean(widened * widened, axis=-1, keepdims=True) + EPSILON)
    return (widened * factor * widened.shape[-1] ** (-0.5)).astype(BF16)


ORDER = ((0, 0), (1, 0), (2, 0), (1, 1), (0, 1), (2, 1), (3, 0), (3, 1))
PLACE = {block: place for place, block in enumerate(ORDER)}
OWN_STAGES = (
    ((0, 0), (1, 0), (0, 1), (2, 0), (1, 1)),
    ((3, 0), (2, 1)),
    (),
    ((3, 1),),
    (),
)
OTHER_STAGES = (
    ((0, 0), (1, 0), (0, 1)),
    ((2, 0), (1, 1)),
    ((3, 0), (2, 1)),
    (),
    ((3, 1),),
)


def runs_of(places):
    found = []
    for place in sorted(places):
        if found and found[-1][1] == place:
            found[-1][1] = place + 1
        else:
            found.append([place, place + 1])
    return found


def stage_tasks(stage):
    here, before = set(), set()
    for at_stage in range(stage + 1):
        before = set(here)
        blocks = [set(sum(names[: at_stage + 1], ())) for names in (OWN_STAGES, OTHER_STAGES)]
        for target in blocks[0]:
            for side in (0, 1):
                for source in blocks[side]:
                    if (target[0], source[1]) in blocks[side]:
                        here.add((PLACE[target], side * 8 + PLACE[source]))
    new = here - before
    targets = sorted({target for target, _ in new})
    return [(one, runs_of([source for target, source in new if target == one])) for one in targets]


def dot_nt(lhs, rhs):
    return lax.dot_general(lhs, rhs, (((1,), (1,)), ((), ())), preferred_element_type=F32)


def dot_nn(lhs, rhs):
    return lax.dot_general(lhs, rhs, (((1,), (0,)), ((), ())), preferred_element_type=F32)


def payload_kernel(count_ref, emb_in, list_in, out_ref, emb_ref, list_ref, sems):
    rows = emb_ref.shape[0]
    width = emb_ref.shape[1]
    slots = list_ref.shape[1]
    emb_copy = pltpu.make_async_copy(emb_in, emb_ref, sems.at[0])
    list_copy = pltpu.make_async_copy(list_in, list_ref, sems.at[1])
    emb_copy.start()
    list_copy.start()
    emb_copy.wait()
    list_copy.wait()
    out_ref[0:rows, :] = normalize(emb_ref[...])
    live = lax.broadcasted_iota(jnp.int32, (1, slots), 1) < count_ref[0, 0]
    col_hot = (lax.broadcasted_iota(jnp.int32, (EXTRA_ROWS, slots), 0) == list_ref[1:2, :]) & live
    row_hot = lax.broadcasted_iota(jnp.int32, (width, slots), 0) == list_ref[0:1, :]
    table = dot_nt(col_hot.astype(F32).astype(BF16), row_hot.astype(F32).astype(BF16))
    out_ref[rows : rows + EXTRA_ROWS, :] = table.astype(BF16)


def restart_kernel(me_ref, seeds_ref, out_ref, counts):
    seed_cols = seeds_ref.shape[0]
    tiles = counts.shape[1]
    me = me_ref[0]
    spot = lax.broadcasted_iota(jnp.int32, (tiles, TILE), 0)
    offset = spot // 16
    for place, (z, x) in enumerate(ORDER):
        offset = offset + jnp.where((spot // 2) % 8 == place, 4 * z + 2 * x, 0)
    tile_ids = (me ^ offset) * 2 + spot % 2
    lows = lax.broadcasted_iota(jnp.int32, (TILE, TILE), 0)

    @pl.loop(0, seed_cols, unroll=16)
    def _(k):
        row = seeds_ref[pl.ds(k, 1), :]
        high_hot = (tile_ids == row // TILE).astype(F32).astype(BF16)
        low_hot = (lows == row % TILE).astype(F32).astype(BF16)
        counts[k] = dot_nt(high_hot, low_hot) * float(SEED_SHARE)

    for t in range(tiles):
        out_ref[0:seed_cols, t * TILE : (t + 1) * TILE] = counts[:, t, :].astype(BF16)
    rest = out_ref.shape[0] - seed_cols
    first = lax.broadcasted_iota(jnp.int32, (rest, out_ref.shape[1]), 0) == 0
    out_ref[seed_cols:, :] = first.astype(F32).astype(BF16)


def stage_kernel(stage, me_ref, rt_ref, *refs):
    own_names, other_names = OWN_STAGES[stage], OTHER_STAGES[stage]
    count = len(own_names) + len(other_names)
    arrivals, refs = refs[:count], refs[count:]
    if stage > 0:
        refs = refs[4 if stage == len(OWN_STAGES) - 1 else 5 :]
    units, bias, kt_ref, total_ref = refs[:4]
    refs = refs[4:]
    me = me_ref[0]
    core, x_pos, z_pos = me % 2, (me // 2) % 2, me // 4
    rows = units.shape[0] // 16
    names = [(0, one) for one in own_names] + [(1, one) for one in other_names]
    for (side, one), ref in zip(names, arrivals):
        place = side * 8 + PLACE[one]
        units[place * rows : (place + 1) * rows] = ref[0:rows]
    if names:
        pick_row = lax.broadcasted_iota(jnp.int32, (TILE, 4 * TILE), 0)
        pick_col = lax.broadcasted_iota(jnp.int32, (TILE, 4 * TILE), 1) // TILE
        wanted = 4 * (x_pos ^ (pick_col // 2)) + 2 * core + pick_col % 2
        pick = (pick_row == wanted).astype(F32).astype(BF16)
        tables = jnp.concatenate(
            [ref[rows : rows + EXTRA_ROWS, 0:TILE] for ref in arrivals], axis=0
        )
        live = jnp.where(dot_nn(tables, pick) > 0.5, -SLOPE, DEAD)
        for at, (side, (z, x)) in enumerate(names):
            group = (side * 2 + x) * 8
            for xs in range(2):
                lane = PLACE[(z, xs)] * rows
                bias[group : group + 8, lane : lane + rows] = live[
                    at * EXTRA_ROWS : at * EXTRA_ROWS + 8, xs * rows : (xs + 1) * rows
                ]
    if stage == 0:
        total_ref[...] = jnp.zeros_like(total_ref)
    for target, spans in stage_tasks(stage):
        lanes = slice(target * rows, (target + 1) * rows)
        for low, high in spans:
            inner = dot_nt(units[low * rows : high * rows, :], units[lanes, :])
            for tile in range((high - low) * rows // TILE):
                source = low + tile // 2
                z, x = ORDER[source % 8]
                bias_row = (source // 8 * 2 + x) * 8 + 2 * (z_pos ^ z) + tile % 2
                shift = bias[pl.ds(bias_row, 1), lanes]
                value = jnp.exp2(inner[tile * TILE : (tile + 1) * TILE] * SLOPE + shift)
                kt_ref[low * rows + tile * TILE : low * rows + (tile + 1) * TILE, lanes] = value.astype(BF16)
        total = total_ref[:, lanes]
        for low, high in spans:
            total = total + dot_nn(rt_ref[:, low * rows : high * rows], kt_ref[low * rows : high * rows, lanes])
        total_ref[:, lanes] = total
    if stage < len(OWN_STAGES) - 1:
        refs[0][...] = jnp.zeros_like(refs[0])
        return
    next_ref, gain_ref = refs
    seed_cols = next_ref.shape[0]
    chunk = 512
    for c in range(next_ref.shape[1] // chunk):
        lanes = slice(c * chunk, (c + 1) * chunk)
        gain = DAMPING / total_ref[seed_cols : seed_cols + 8, lanes]
        gain_ref[:, lanes] = gain
        next_ref[:, lanes] = (
            (1.0 - DAMPING) * rt_ref[0:seed_cols, lanes].astype(F32) + total_ref[0:seed_cols, lanes] * gain[0:1]
        ).astype(BF16)


def padded(ranks):
    return jnp.concatenate([ranks, jnp.zeros_like(ranks)], axis=0)


def half_kernel(kt_ref, mine_ref, out_ref):
    seed_cols, own = mine_ref.shape
    mine = padded(mine_ref[...])
    chunk = 512
    for c in range(own // chunk):
        lanes = slice(c * chunk, (c + 1) * chunk)
        out_ref[:, lanes] = dot_nn(mine, kt_ref[0:own, lanes])[0:seed_cols]


def step_kernel(rt_ref, kt_ref, gain_ref, half_ref, other_ref, out_ref):
    seed_cols, own = out_ref.shape
    other = padded(other_ref[...])
    chunk = 512
    for c in range(own // chunk):
        lanes = slice(c * chunk, (c + 1) * chunk)
        total = half_ref[:, lanes] + dot_nn(other, kt_ref[own:, lanes])[0:seed_cols]
        out_ref[:, lanes] = (
            (1.0 - DAMPING) * rt_ref[0:seed_cols, lanes].astype(F32) + total * gain_ref[0:1, lanes]
        ).astype(BF16)


def last_kernel(rt_ref, kt_ref, gain_ref, mine_ref, other_ref, out_ref):
    seed_cols, rows = out_ref.shape
    own = mine_ref.shape[1]
    total = dot_nn(padded(mine_ref[...]), kt_ref[0:own, 0:rows]) + dot_nn(
        padded(other_ref[...]), kt_ref[own:, 0:rows]
    )
    out_ref[...] = (1.0 - DAMPING) * rt_ref[0:seed_cols, 0:rows].astype(F32) + total[
        0:seed_cols
    ] * gain_ref[0:1, 0:rows]


WHOLE = pl.BlockSpec(memory_space=pltpu.VMEM)
SCALARS = pl.BlockSpec(memory_space=pltpu.SMEM)
REMAIN = pl.BlockSpec(memory_space=pl.ANY)


def params():
    return pltpu.CompilerParams(vmem_limit_bytes=20 * 2**20)


def work(micros):
    return pl.CostEstimate(flops=int(micros * 1e9), bytes_accessed=int(micros * 3e6), transcendentals=0)


def swap(array, mapping):
    pairs = [(device, mapping(device)) for device in range(16)]
    return lax.ppermute(array, ("row", "col"), pairs)


def near(device):
    return device ^ 4


def far(device):
    return device ^ 8


def across(device):
    return device ^ 2


def sibling(device):
    return device ^ 1


def chip_local(embeddings, tile_list, tile_count, seeds):
    row_pos = lax.axis_index("row")
    me = (row_pos * 4 + lax.axis_index("col")).reshape(1)
    rows, width = embeddings.shape
    seed_cols = seeds.shape[0]
    sessions = rows * 16
    own = rows * 8
    slots = tile_list.shape[3]
    block = pl.pallas_call(
        payload_kernel,
        in_specs=[SCALARS, REMAIN, REMAIN],
        out_specs=WHOLE,
        out_shape=jax.ShapeDtypeStruct((rows + EXTRA_ROWS, width), BF16),
        scratch_shapes=[
            pltpu.VMEM((rows, width), BF16),
            pltpu.VMEM((2, slots), jnp.int32),
            pltpu.SemaphoreType.DMA((2,)),
        ],
        compiler_params=params(),
        name="payload",
    )(tile_count, embeddings, tile_list.reshape(2, slots))

    state_shapes = [
        pltpu.VMEM((sessions, width), BF16),
        pltpu.VMEM((32, own), F32),
        pltpu.VMEM((sessions, own), BF16),
        pltpu.VMEM((2 * seed_cols, own), F32),
    ]
    mark = [jax.ShapeDtypeStruct((8, TILE), F32)]

    def run_stage(stage, rt, arrivals, state, extra, *after):
        first_state = 2 + len(arrivals)
        outs = pl.pallas_call(
            functools.partial(stage_kernel, stage),
            in_specs=[SCALARS] + [WHOLE] * (1 + len(arrivals) + len(state)) + [REMAIN] * len(after),
            out_specs=[WHOLE] * (4 + len(extra)),
            out_shape=state_shapes + extra,
            input_output_aliases={first_state + k: k for k in range(len(state))},
            compiler_params=params(),
            cost_estimate=work(2.5),
            name=f"stage{stage}",
        )(me, rt, *arrivals, *state, *after)
        return outs[:4], outs[4:]

    z2 = swap(block, far)
    z1 = swap(block, near)
    x0 = swap(block, across)
    b00 = swap(block, sibling)
    x1 = swap(z1, across)
    b10 = swap(z1, sibling)
    b01 = swap(x0, sibling)
    seeds, z1, x0 = lax.optimization_barrier((seeds, z1, x0))
    rt = pl.pallas_call(
        restart_kernel,
        in_specs=[SCALARS, WHOLE],
        out_specs=WHOLE,
        out_shape=jax.ShapeDtypeStruct((2 * seed_cols, sessions), BF16),
        scratch_shapes=[pltpu.VMEM((seed_cols, sessions // TILE, TILE), F32)],
        compiler_params=params(),
        cost_estimate=work(2.6),
        name="restart",
    )(me, seeds)
    z2, x1, b00, b10, b01, rt = lax.optimization_barrier((z2, x1, b00, b10, b01, rt))
    z3 = swap(z2, near)
    x2 = swap(z2, across)
    b20 = swap(z2, sibling)
    b11 = swap(x1, sibling)
    state, (done,) = run_stage(0, rt, [block, z1, x0, z2, x1, b00, b10, b01], [], mark)
    z3, x2, done = lax.optimization_barrier((z3, x2, done))
    x3 = swap(z3, across)
    b30 = swap(z3, sibling)
    b21 = swap(x2, sibling)
    state, (done,) = run_stage(1, rt, [z3, x2, b20, b11], state, mark, done)
    state, (done,) = run_stage(2, rt, [b30, b21], state, mark, done)
    x3, done = lax.optimization_barrier((x3, done))
    b31 = swap(x3, sibling)
    state, (done,) = run_stage(3, rt, [x3], state, mark, done)
    state, (ranks, gain) = run_stage(
        4,
        rt,
        [b31],
        state,
        [jax.ShapeDtypeStruct((seed_cols, own), BF16), jax.ShapeDtypeStruct((8, own), F32)],
    )
    kt = state[2]
    for sweep in range(ITERS - 2):
        half = pl.pallas_call(
            half_kernel,
            in_specs=[WHOLE] * 2,
            out_specs=WHOLE,
            out_shape=jax.ShapeDtypeStruct((seed_cols, own), F32),
            compiler_params=params(),
            cost_estimate=work(1.5),
            name="half",
        )(kt, ranks)
        ranks = pl.pallas_call(
            step_kernel,
            in_specs=[WHOLE] * 5,
            out_specs=WHOLE,
            out_shape=jax.ShapeDtypeStruct((seed_cols, own), BF16),
            compiler_params=params(),
            cost_estimate=work(1.5),
            name="step",
        )(rt, kt, gain, half, swap(ranks, sibling))
    result = pl.pallas_call(
        last_kernel,
        in_specs=[WHOLE] * 5,
        out_specs=WHOLE,
        out_shape=jax.ShapeDtypeStruct((seed_cols, rows), F32),
        compiler_params=params(),
        cost_estimate=work(0.5),
        name="last",
    )(rt, kt, gain, ranks, swap(ranks, sibling))
    return result.T


def block_width():
    for option_width in (16, 8, 4, 2):
        return option_width
    return 1


def seed_mass(seed_index, is_valid, length):
    spots = jnp.arange(length, dtype=jnp.int32)

    def one_column(pieces):
        index_row, valid_row = pieces
        hits = (index_row[:, None] == spots[None, :]) & valid_row[:, None]
        return jnp.sum(hits.astype(jnp.float32), axis=0) * float(SEED_SHARE)

    table = lax.map(one_column, (seed_index, is_valid))
    return table.T


def grid_local(embeddings, tile_list, tile_count, seeds):
    n_row = lax.axis_size("row")
    n_col = lax.axis_size("col")
    row_pos = lax.axis_index("row")
    col_pos = lax.axis_index("col")
    slice_rows = embeddings.shape[0]
    grid_rows = slice_rows * n_col
    row_tiles = grid_rows // TILE
    col_tiles = slice_rows * n_row // TILE
    seed_cols = seeds.shape[0]
    unit_rows = normalize(embeddings)
    row_emb = lax.all_gather(unit_rows, "col", axis=0, tiled=True).reshape(row_tiles, TILE, -1)
    col_emb = lax.all_gather(unit_rows, "row", axis=0, tiled=True).reshape(col_tiles, TILE, -1)
    slots = tile_list.shape[3]
    width_b = block_width()
    turn_count = slots // width_b
    row_ids = tile_list[0, 0, 0]
    col_ids = tile_list[0, 0, 1]
    live_mask = (jnp.arange(slots, dtype=jnp.int32) < tile_count[0, 0]).astype(jnp.float32)
    row_blocks = row_ids.reshape(turn_count, width_b)
    col_blocks = col_ids.reshape(turn_count, width_b)
    live_blocks = live_mask.reshape(turn_count, width_b)

    def kernel_turn(degree, pieces):
        row_part, col_part, live_part = pieces
        left_tiles = jnp.take(row_emb, row_part, axis=0)
        right_tiles = jnp.take(col_emb, col_part, axis=0)
        inner_prod = jnp.einsum(
            "bie,bje->bij", left_tiles, right_tiles, preferred_element_type=jnp.float32
        )
        values = jnp.exp(KERNEL_GAIN * (2.0 * inner_prod - 2.0)).astype(jnp.bfloat16)
        row_total = jnp.sum(values.astype(jnp.float32), axis=2)
        degree = degree.at[row_part].add(row_total * live_part[:, None])
        return (degree, values)

    degree_part, kernel = lax.scan(
        kernel_turn,
        jnp.zeros((row_tiles, TILE), jnp.float32),
        (row_blocks, col_blocks, live_blocks),
    )
    degree_part = degree_part.reshape(grid_rows)

    def spread(ranks_col):
        col_ranks = ranks_col.reshape(col_tiles, TILE, seed_cols)

        def rank_turn(running, pieces):
            row_part, col_part, live_part, values = pieces
            right_tiles = jnp.take(col_ranks, col_part, axis=0)
            product = jnp.einsum(
                "bij,bjk->bik", values, right_tiles, preferred_element_type=jnp.float32
            )
            running = running.at[row_part].add(product * live_part[:, None, None])
            return (running, None)

        running, unused = lax.scan(
            rank_turn,
            jnp.zeros((row_tiles, TILE, seed_cols), jnp.float32),
            (row_blocks, col_blocks, live_blocks, kernel),
        )
        return running.reshape(grid_rows, seed_cols)

    own_start = (row_pos * n_col + col_pos) * slice_rows
    own_index = seeds - own_start
    seed_own = seed_mass(own_index, (own_index >= 0) & (own_index < slice_rows), slice_rows)
    degree = lax.psum_scatter(degree_part, "col", scatter_dimension=0, tiled=True)
    opening = lax.all_gather(seed_own.astype(jnp.bfloat16), "row", axis=0, tiled=True)
    partial_rows = spread(opening)
    summed = lax.psum_scatter(partial_rows, "col", scatter_dimension=0, tiled=True)
    rank_rows = (1.0 - DAMPING) * seed_own + DAMPING * summed / degree[:, None]
    for sweep_idx in range(ITERS - 1):
        gathered = lax.all_gather(rank_rows.astype(jnp.bfloat16), "row", axis=0, tiled=True)
        partial_rows = spread(gathered)
        summed = lax.psum_scatter(partial_rows, "col", scatter_dimension=0, tiled=True)
        rank_rows = (1.0 - DAMPING) * seed_own + DAMPING * summed / degree[:, None]
    return rank_rows


def solution(mesh):
    n_row, n_col = mesh.shape["row"], mesh.shape["col"]

    def local(embeddings, tile_list, tile_count, seeds):
        small = n_row == 4 and n_col == 4 and embeddings.shape == (2 * TILE, 2 * TILE)
        if small and seeds.shape == (64, TILE):
            return chip_local(embeddings, tile_list, tile_count, seeds)
        return grid_local(embeddings, tile_list, tile_count, seeds)

    return jax.shard_map(
        local,
        mesh=mesh,
        in_specs=(
            P(("groups", "row", "col"), None),
            P(("groups", "row"), "col", None, None),
            P(("groups", "row"), "col"),
            P("groups", None),
        ),
        out_specs=P(("groups", "row", "col"), None),
        check_vma=False,
    )
```

```python
import functools
import math

import jax
import jax.numpy as jnp
from jax import lax
from jax.experimental import pallas as pl
from jax.experimental.pallas import tpu as pltpu
from jax.sharding import PartitionSpec as P

TILE = 128
ITERS = 3
SEED_SHARE = 32


KERNEL_GAIN = 4.0
DAMPING = 0.85
EPSILON = 1e-06

SLOPE = 2.0 * KERNEL_GAIN * math.log2(math.e)
DEAD = -1e9
MASK_ROWS = 16
EXTRA_ROWS = 16

F32 = jnp.float32
BF16 = jnp.bfloat16


def normalize(rows_in):
    widened = rows_in.astype(F32)
    factor = lax.rsqrt(jnp.mean(widened * widened, axis=-1, keepdims=True) + EPSILON)
    return (widened * factor * widened.shape[-1] ** (-0.5)).astype(BF16)


ORDER = ((0, 0), (1, 0), (2, 0), (0, 1), (1, 1), (2, 1), (3, 0), (3, 1))
PLACE = {block: place for place, block in enumerate(ORDER)}
OWN_STAGES = (
    ((0, 0), (1, 0), (0, 1), (2, 0), (1, 1)),
    ((3, 0), (2, 1)),
    (),
    ((3, 1),),
    (),
)
OTHER_STAGES = (
    ((0, 0), (1, 0)),
    ((0, 1), (2, 0), (1, 1)),
    ((3, 0), (2, 1)),
    (),
    ((3, 1),),
)


def runs_of(places):
    found = []
    for place in sorted(places):
        if found and found[-1][1] == place:
            found[-1][1] = place + 1
        else:
            found.append([place, place + 1])
    return found


def stage_tasks(stage):
    here, before = set(), set()
    for at_stage in range(stage + 1):
        before = set(here)
        blocks = [set(sum(names[: at_stage + 1], ())) for names in (OWN_STAGES, OTHER_STAGES)]
        for target in blocks[0]:
            for side in (0, 1):
                for source in blocks[side]:
                    if (target[0], source[1]) in blocks[side]:
                        here.add((PLACE[target], side * 8 + PLACE[source]))
    wanted = {}
    for target, source in here - before:
        wanted.setdefault(target, set()).add(source)
    tasks = []
    for sources in sorted({tuple(sorted(one)) for one in wanted.values()}):
        for low, high in runs_of([target for target in wanted if tuple(sorted(wanted[target])) == sources]):
            tasks.append((low, high, runs_of(sources)))
    return tasks


def dot_nt(lhs, rhs):
    return lax.dot_general(lhs, rhs, (((1,), (1,)), ((), ())), preferred_element_type=F32)


def dot_nn(lhs, rhs):
    return lax.dot_general(lhs, rhs, (((1,), (0,)), ((), ())), preferred_element_type=F32)


def payload_kernel(count_ref, emb_in, list_in, seeds_in, out_ref, seeds_ref, emb_ref, list_ref, sems):
    rows = emb_ref.shape[0]
    width = emb_ref.shape[1]
    slots = list_ref.shape[1]
    emb_copy = pltpu.make_async_copy(emb_in, emb_ref, sems.at[0])
    list_copy = pltpu.make_async_copy(list_in, list_ref, sems.at[1])
    seeds_copy = pltpu.make_async_copy(seeds_in, seeds_ref, sems.at[2])
    emb_copy.start()
    list_copy.start()
    seeds_copy.start()
    emb_copy.wait()
    list_copy.wait()
    out_ref[0:rows, :] = normalize(emb_ref[...])
    live = lax.broadcasted_iota(jnp.int32, (1, slots), 1) < count_ref[0, 0]
    col_hot = (lax.broadcasted_iota(jnp.int32, (EXTRA_ROWS, slots), 0) == list_ref[1:2, :]) & live
    row_hot = lax.broadcasted_iota(jnp.int32, (width, slots), 0) == list_ref[0:1, :]
    table = dot_nt(col_hot.astype(F32).astype(BF16), row_hot.astype(F32).astype(BF16))
    out_ref[rows : rows + EXTRA_ROWS, :] = table.astype(BF16)
    seeds_copy.wait()


def restart_kernel(me_ref, seeds_ref, out_ref, counts):
    seed_cols = seeds_ref.shape[0]
    tiles = counts.shape[1]
    me = me_ref[0]
    spot = lax.broadcasted_iota(jnp.int32, (tiles, TILE), 0)
    offset = spot // 16
    for place, (z, x) in enumerate(ORDER):
        offset = offset + jnp.where((spot // 2) % 8 == place, 4 * z + 2 * x, 0)
    tile_ids = (me ^ offset) * 2 + spot % 2
    lows = lax.broadcasted_iota(jnp.int32, (TILE, TILE), 0)

    @pl.loop(0, seed_cols, unroll=16)
    def _(k):
        row = seeds_ref[pl.ds(k, 1), :]
        high_hot = (tile_ids == row // TILE).astype(F32).astype(BF16)
        low_hot = (lows == row % TILE).astype(F32).astype(BF16)
        counts[k] = dot_nt(high_hot, low_hot) * float(SEED_SHARE)

    for t in range(tiles):
        out_ref[0:seed_cols, t * TILE : (t + 1) * TILE] = counts[:, t, :].astype(BF16)
    rest = out_ref.shape[0] - seed_cols
    first = lax.broadcasted_iota(jnp.int32, (rest, out_ref.shape[1]), 0) == 0
    out_ref[seed_cols:, :] = first.astype(F32).astype(BF16)


def stage_kernel(stage, me_ref, rt_ref, *refs):
    own_names, other_names = OWN_STAGES[stage], OTHER_STAGES[stage]
    count = len(own_names) + len(other_names)
    arrivals, refs = refs[:count], refs[count:]
    if stage > 0:
        refs = refs[4 if stage == len(OWN_STAGES) - 1 else 5 :]
    units, bias, kt_ref, total_ref = refs[:4]
    refs = refs[4:]
    me = me_ref[0]
    core, x_pos, z_pos = me % 2, (me // 2) % 2, me // 4
    rows = units.shape[0] // 16
    names = [(0, one) for one in own_names] + [(1, one) for one in other_names]
    for (side, one), ref in zip(names, arrivals):
        place = side * 8 + PLACE[one]
        units[place * rows : (place + 1) * rows] = ref[0:rows]
    if names:
        pick_row = lax.broadcasted_iota(jnp.int32, (TILE, 4 * TILE), 0)
        pick_col = lax.broadcasted_iota(jnp.int32, (TILE, 4 * TILE), 1) // TILE
        wanted = 4 * (x_pos ^ (pick_col // 2)) + 2 * core + pick_col % 2
        pick = (pick_row == wanted).astype(F32).astype(BF16)
        tables = jnp.concatenate(
            [ref[rows : rows + EXTRA_ROWS, 0:TILE] for ref in arrivals], axis=0
        )
        live = jnp.where(dot_nn(tables, pick) > 0.5, -SLOPE, DEAD)
        for at, (side, (z, x)) in enumerate(names):
            group = (side * 2 + x) * 8
            for xs in range(2):
                lane = PLACE[(z, xs)] * rows
                bias[group : group + 8, lane : lane + rows] = live[
                    at * EXTRA_ROWS : at * EXTRA_ROWS + 8, xs * rows : (xs + 1) * rows
                ]
    if stage == 0:
        total_ref[...] = jnp.zeros_like(total_ref)
    tasks = stage_tasks(stage)
    for first, end, spans in tasks:
        lanes = slice(first * rows, end * rows)
        for low, high in spans:
            inner = dot_nt(units[low * rows : high * rows, :], units[lanes, :])
            for tile in range((high - low) * rows // TILE):
                source = low + tile // 2
                z, x = ORDER[source % 8]
                bias_row = (source // 8 * 2 + x) * 8 + 2 * (z_pos ^ z) + tile % 2
                shift = bias[pl.ds(bias_row, 1), lanes]
                value = jnp.exp2(inner[tile * TILE : (tile + 1) * TILE] * SLOPE + shift)
                kt_ref[low * rows + tile * TILE : low * rows + (tile + 1) * TILE, lanes] = value.astype(BF16)
    kept = total_ref.shape[0]
    for first, end, spans in tasks:
        lanes = slice(first * rows, end * rows)
        total = total_ref[:, lanes]
        for low, high in spans:
            sources = slice(low * rows, high * rows)
            total = total + dot_nn(rt_ref[:, sources], kt_ref[sources, lanes])[0:kept]
        total_ref[:, lanes] = total
    if stage < len(OWN_STAGES) - 1:
        refs[0][...] = jnp.zeros_like(refs[0])
        return
    next_ref, gain_ref = refs
    seed_cols = next_ref.shape[0]
    chunk = 512
    for c in range(next_ref.shape[1] // chunk):
        lanes = slice(c * chunk, (c + 1) * chunk)
        gain = DAMPING / total_ref[seed_cols : seed_cols + 8, lanes]
        gain_ref[:, lanes] = gain
        next_ref[:, lanes] = (
            (1.0 - DAMPING) * rt_ref[0:seed_cols, lanes].astype(F32) + total_ref[0:seed_cols, lanes] * gain[0:1]
        ).astype(BF16)


def padded(ranks):
    return jnp.concatenate([ranks, jnp.zeros_like(ranks)], axis=0)


def half_kernel(kt_ref, mine_ref, out_ref):
    seed_cols, own = mine_ref.shape
    mine = padded(mine_ref[...])
    chunk = 512
    for c in range(own // chunk):
        lanes = slice(c * chunk, (c + 1) * chunk)
        out_ref[:, lanes] = dot_nn(mine, kt_ref[0:own, lanes])[0:seed_cols]


def step_kernel(rt_ref, kt_ref, gain_ref, half_ref, other_ref, out_ref):
    seed_cols, own = out_ref.shape
    other = padded(other_ref[...])
    chunk = 512
    for c in range(own // chunk):
        lanes = slice(c * chunk, (c + 1) * chunk)
        total = half_ref[:, lanes] + dot_nn(other, kt_ref[own:, lanes])[0:seed_cols]
        out_ref[:, lanes] = (
            (1.0 - DAMPING) * rt_ref[0:seed_cols, lanes].astype(F32) + total * gain_ref[0:1, lanes]
        ).astype(BF16)


def last_kernel(rt_ref, kt_ref, gain_ref, mine_ref, other_ref, out_ref):
    seed_cols, rows = out_ref.shape
    own = mine_ref.shape[1]
    total = dot_nn(padded(mine_ref[...]), kt_ref[0:own, 0:rows]) + dot_nn(
        padded(other_ref[...]), kt_ref[own:, 0:rows]
    )
    out_ref[...] = (1.0 - DAMPING) * rt_ref[0:seed_cols, 0:rows].astype(F32) + total[
        0:seed_cols
    ] * gain_ref[0:1, 0:rows]


WHOLE = pl.BlockSpec(memory_space=pltpu.VMEM)
SCALARS = pl.BlockSpec(memory_space=pltpu.SMEM)
REMAIN = pl.BlockSpec(memory_space=pl.ANY)


def params():
    return pltpu.CompilerParams(vmem_limit_bytes=20 * 2**20)


def in_hbm(array):
    return pltpu.with_memory_space_constraint(array, pltpu.HBM)


def work(micros):
    return pl.CostEstimate(flops=int(micros * 1000), bytes_accessed=int(micros * 100), transcendentals=0)


def swap(array, mapping):
    pairs = [(device, mapping(device)) for device in range(16)]
    return lax.ppermute(array, ("row", "col"), pairs)


def near(device):
    return device ^ 4


def far(device):
    return device ^ 8


def across(device):
    return device ^ 2


def sibling(device):
    return device ^ 1


def chip_local(embeddings, tile_list, tile_count, seeds):
    row_pos = lax.axis_index("row")
    me = (row_pos * 4 + lax.axis_index("col")).reshape(1)
    rows, width = embeddings.shape
    seed_cols = seeds.shape[0]
    sessions = rows * 16
    own = rows * 8
    slots = tile_list.shape[3]
    block, seeds = pl.pallas_call(
        payload_kernel,
        in_specs=[SCALARS] + [REMAIN] * 3,
        out_specs=[WHOLE] * 2,
        out_shape=[
            pltpu.VMEM((rows + EXTRA_ROWS, width), BF16),
            pltpu.VMEM(seeds.shape, seeds.dtype),
        ],
        scratch_shapes=[
            pltpu.VMEM((rows, width), BF16),
            pltpu.VMEM((2, slots), jnp.int32),
            pltpu.SemaphoreType.DMA((3,)),
        ],
        compiler_params=params(),
        name="payload",
    )(tile_count, in_hbm(embeddings), in_hbm(tile_list.reshape(2, slots)), in_hbm(seeds))
    state_shapes = [
        pltpu.VMEM((sessions, width), BF16),
        pltpu.VMEM((32, own), F32),
        pltpu.VMEM((sessions, own), BF16),
        pltpu.VMEM((seed_cols + 8, own), F32),
    ]
    mark = [jax.ShapeDtypeStruct((8, TILE), F32)]

    def run_stage(stage, rt, arrivals, state, extra, *after):
        first_state = 2 + len(arrivals)
        outs = pl.pallas_call(
            functools.partial(stage_kernel, stage),
            in_specs=[SCALARS] + [WHOLE] * (1 + len(arrivals) + len(state)) + [REMAIN] * len(after),
            out_specs=[WHOLE] * (4 + len(extra)),
            out_shape=state_shapes + extra,
            input_output_aliases={first_state + k: k for k in range(len(state))},
            compiler_params=params(),
            cost_estimate=work(2.5),
            name=f"stage{stage}",
        )(me, rt, *arrivals, *state, *after)
        return outs[:4], outs[4:]

    z1 = swap(block, near)
    z2 = swap(block, far)
    x0 = swap(block, across)
    b00 = swap(block, sibling)
    rt = pl.pallas_call(
        restart_kernel,
        in_specs=[SCALARS, WHOLE],
        out_specs=WHOLE,
        out_shape=jax.ShapeDtypeStruct((2 * seed_cols, sessions), BF16),
        scratch_shapes=[pltpu.VMEM((seed_cols, sessions // TILE, TILE), F32)],
        compiler_params=params(),
        cost_estimate=work(2.6),
        name="restart",
    )(me, seeds)
    z1, rt = lax.optimization_barrier((z1, rt))
    x1 = swap(z1, across)
    b10 = swap(z1, sibling)
    x0, z2, b00 = lax.optimization_barrier((x0, z2, b00))
    z3 = swap(z2, near)
    x2 = swap(z2, across)
    b20 = swap(z2, sibling)
    b01 = swap(x0, sibling)
    b11 = swap(x1, sibling)
    state, (done,) = run_stage(0, rt, [block, z1, x0, z2, x1, b00, b10], [], mark)
    x2, z3, done = lax.optimization_barrier((x2, z3, done))
    x3 = swap(z3, across)
    b30 = swap(z3, sibling)
    b21 = swap(x2, sibling)
    state, (done,) = run_stage(1, rt, [z3, x2, b01, b20, b11], state, mark, done)
    state, (done,) = run_stage(2, rt, [b30, b21], state, mark, done)
    x3, done = lax.optimization_barrier((x3, done))
    b31 = swap(x3, sibling)
    state, (done,) = run_stage(3, rt, [x3], state, mark, done)
    state, (ranks, gain) = run_stage(
        4,
        rt,
        [b31],
        state,
        [jax.ShapeDtypeStruct((seed_cols, own), BF16), jax.ShapeDtypeStruct((8, own), F32)],
    )
    kt = state[2]
    for sweep in range(ITERS - 2):
        half = pl.pallas_call(
            half_kernel,
            in_specs=[WHOLE] * 2,
            out_specs=WHOLE,
            out_shape=jax.ShapeDtypeStruct((seed_cols, own), F32),
            compiler_params=params(),
            cost_estimate=work(1.5),
            name="half",
        )(kt, ranks)
        ranks = pl.pallas_call(
            step_kernel,
            in_specs=[WHOLE] * 5,
            out_specs=WHOLE,
            out_shape=jax.ShapeDtypeStruct((seed_cols, own), BF16),
            compiler_params=params(),
            cost_estimate=work(1.5),
            name="step",
        )(rt, kt, gain, half, swap(ranks, sibling))
    result = pl.pallas_call(
        last_kernel,
        in_specs=[WHOLE] * 5,
        out_specs=WHOLE,
        out_shape=jax.ShapeDtypeStruct((seed_cols, rows), F32),
        compiler_params=params(),
        cost_estimate=work(0.5),
        name="last",
    )(rt, kt, gain, ranks, swap(ranks, sibling))
    return result.T


def block_width():
    for option_width in (16, 8, 4, 2):
        return option_width
    return 1


def seed_mass(seed_index, is_valid, length):
    spots = jnp.arange(length, dtype=jnp.int32)

    def one_column(pieces):
        index_row, valid_row = pieces
        hits = (index_row[:, None] == spots[None, :]) & valid_row[:, None]
        return jnp.sum(hits.astype(jnp.float32), axis=0) * float(SEED_SHARE)

    table = lax.map(one_column, (seed_index, is_valid))
    return table.T


def grid_local(embeddings, tile_list, tile_count, seeds):
    n_row = lax.axis_size("row")
    n_col = lax.axis_size("col")
    row_pos = lax.axis_index("row")
    col_pos = lax.axis_index("col")
    slice_rows = embeddings.shape[0]
    grid_rows = slice_rows * n_col
    row_tiles = grid_rows // TILE
    col_tiles = slice_rows * n_row // TILE
    seed_cols = seeds.shape[0]
    unit_rows = normalize(embeddings)
    row_emb = lax.all_gather(unit_rows, "col", axis=0, tiled=True).reshape(row_tiles, TILE, -1)
    col_emb = lax.all_gather(unit_rows, "row", axis=0, tiled=True).reshape(col_tiles, TILE, -1)
    slots = tile_list.shape[3]
    width_b = block_width()
    turn_count = slots // width_b
    row_ids = tile_list[0, 0, 0]
    col_ids = tile_list[0, 0, 1]
    live_mask = (jnp.arange(slots, dtype=jnp.int32) < tile_count[0, 0]).astype(jnp.float32)
    row_blocks = row_ids.reshape(turn_count, width_b)
    col_blocks = col_ids.reshape(turn_count, width_b)
    live_blocks = live_mask.reshape(turn_count, width_b)

    def kernel_turn(degree, pieces):
        row_part, col_part, live_part = pieces
        left_tiles = jnp.take(row_emb, row_part, axis=0)
        right_tiles = jnp.take(col_emb, col_part, axis=0)
        inner_prod = jnp.einsum(
            "bie,bje->bij", left_tiles, right_tiles, preferred_element_type=jnp.float32
        )
        values = jnp.exp(KERNEL_GAIN * (2.0 * inner_prod - 2.0)).astype(jnp.bfloat16)
        row_total = jnp.sum(values.astype(jnp.float32), axis=2)
        degree = degree.at[row_part].add(row_total * live_part[:, None])
        return (degree, values)

    degree_part, kernel = lax.scan(
        kernel_turn,
        jnp.zeros((row_tiles, TILE), jnp.float32),
        (row_blocks, col_blocks, live_blocks),
    )
    degree_part = degree_part.reshape(grid_rows)

    def spread(ranks_col):
        col_ranks = ranks_col.reshape(col_tiles, TILE, seed_cols)

        def rank_turn(running, pieces):
            row_part, col_part, live_part, values = pieces
            right_tiles = jnp.take(col_ranks, col_part, axis=0)
            product = jnp.einsum(
                "bij,bjk->bik", values, right_tiles, preferred_element_type=jnp.float32
            )
            running = running.at[row_part].add(product * live_part[:, None, None])
            return (running, None)

        running, unused = lax.scan(
            rank_turn,
            jnp.zeros((row_tiles, TILE, seed_cols), jnp.float32),
            (row_blocks, col_blocks, live_blocks, kernel),
        )
        return running.reshape(grid_rows, seed_cols)

    own_start = (row_pos * n_col + col_pos) * slice_rows
    own_index = seeds - own_start
    seed_own = seed_mass(own_index, (own_index >= 0) & (own_index < slice_rows), slice_rows)
    degree = lax.psum_scatter(degree_part, "col", scatter_dimension=0, tiled=True)
    opening = lax.all_gather(seed_own.astype(jnp.bfloat16), "row", axis=0, tiled=True)
    partial_rows = spread(opening)
    summed = lax.psum_scatter(partial_rows, "col", scatter_dimension=0, tiled=True)
    rank_rows = (1.0 - DAMPING) * seed_own + DAMPING * summed / degree[:, None]
    for sweep_idx in range(ITERS - 1):
        gathered = lax.all_gather(rank_rows.astype(jnp.bfloat16), "row", axis=0, tiled=True)
        partial_rows = spread(gathered)
        summed = lax.psum_scatter(partial_rows, "col", scatter_dimension=0, tiled=True)
        rank_rows = (1.0 - DAMPING) * seed_own + DAMPING * summed / degree[:, None]
    return rank_rows


def solution(mesh):
    n_row, n_col = mesh.shape["row"], mesh.shape["col"]

    def local(embeddings, tile_list, tile_count, seeds):
        small = n_row == 4 and n_col == 4 and embeddings.shape == (2 * TILE, 2 * TILE)
        if small and seeds.shape == (64, TILE):
            return chip_local(embeddings, tile_list, tile_count, seeds)
        return grid_local(embeddings, tile_list, tile_count, seeds)

    return jax.shard_map(
        local,
        mesh=mesh,
        in_specs=(
            P(("groups", "row", "col"), None),
            P(("groups", "row"), "col", None, None),
            P(("groups", "row"), "col"),
            P("groups", None),
        ),
        out_specs=P(("groups", "row", "col"), None),
        check_vma=False,
    )
```

```python
import functools
import math

import jax
import jax.numpy as jnp
from jax import lax
from jax.experimental import pallas as pl
from jax.experimental.pallas import tpu as pltpu
from jax.sharding import PartitionSpec as P

TILE = 128
ITERS = 3
SEED_SHARE = 32


KERNEL_GAIN = 4.0
DAMPING = 0.85
EPSILON = 1e-06

SLOPE = 2.0 * KERNEL_GAIN * math.log2(math.e)
DEAD = -1e9
MASK_ROWS = 16
EXTRA_ROWS = 16

F32 = jnp.float32
BF16 = jnp.bfloat16


def normalize(rows_in):
    widened = rows_in.astype(F32)
    factor = lax.rsqrt(jnp.mean(widened * widened, axis=-1, keepdims=True) + EPSILON)
    return (widened * factor * widened.shape[-1] ** (-0.5)).astype(BF16)


ORDER = ((0, 0), (1, 0), (2, 0), (0, 1), (1, 1), (2, 1), (3, 0), (3, 1))
PLACE = {block: place for place, block in enumerate(ORDER)}
OWN_STAGES = (
    ((0, 0), (1, 0), (0, 1)),
    ((2, 0), (1, 1)),
    ((3, 0), (2, 1)),
    ((3, 1),),
    (),
)
OTHER_STAGES = (
    (),
    ((0, 0), (1, 0), (0, 1)),
    (),
    ((2, 0), (1, 1)),
    ((3, 0), (2, 1), (3, 1)),
)


def runs_of(places):
    found = []
    for place in sorted(places):
        if found and found[-1][1] == place:
            found[-1][1] = place + 1
        else:
            found.append([place, place + 1])
    return found


def stage_tasks(stage):
    here, before = set(), set()
    for at_stage in range(stage + 1):
        before = set(here)
        blocks = [set(sum(names[: at_stage + 1], ())) for names in (OWN_STAGES, OTHER_STAGES)]
        for target in blocks[0]:
            for side in (0, 1):
                for source in blocks[side]:
                    if (target[0], source[1]) in blocks[side]:
                        here.add((PLACE[target], side * 8 + PLACE[source]))
        if (0, 0) in blocks[1]:
            here.update((8, PLACE[source]) for source in blocks[0] if (0, source[1]) in blocks[0])
    wanted = {}
    for target, source in here - before:
        wanted.setdefault(target, set()).add(source)
    tasks = []
    for sources in sorted({tuple(sorted(one)) for one in wanted.values()}):
        for low, high in runs_of([target for target in wanted if tuple(sorted(wanted[target])) == sources]):
            tasks.append((low, high, runs_of(sources)))
    return tasks


def dot_nt(lhs, rhs):
    return lax.dot_general(lhs, rhs, (((1,), (1,)), ((), ())), preferred_element_type=F32)


def dot_nn(lhs, rhs):
    return lax.dot_general(lhs, rhs, (((1,), (0,)), ((), ())), preferred_element_type=F32)


def payload_kernel(count_ref, emb_in, list_in, seeds_in, out_ref, seeds_ref, emb_ref, list_ref, sems):
    rows = emb_ref.shape[0]
    width = emb_ref.shape[1]
    slots = list_ref.shape[1]
    emb_copy = pltpu.make_async_copy(emb_in, emb_ref, sems.at[0])
    list_copy = pltpu.make_async_copy(list_in, list_ref, sems.at[1])
    seeds_copy = pltpu.make_async_copy(seeds_in, seeds_ref, sems.at[2])
    emb_copy.start()
    list_copy.start()
    seeds_copy.start()
    emb_copy.wait()
    list_copy.wait()
    out_ref[0:rows, :] = normalize(emb_ref[...])
    live = lax.broadcasted_iota(jnp.int32, (1, slots), 1) < count_ref[0, 0]
    col_hot = (lax.broadcasted_iota(jnp.int32, (EXTRA_ROWS, slots), 0) == list_ref[1:2, :]) & live
    row_hot = lax.broadcasted_iota(jnp.int32, (width, slots), 0) == list_ref[0:1, :]
    table = dot_nt(col_hot.astype(F32).astype(BF16), row_hot.astype(F32).astype(BF16))
    out_ref[rows : rows + EXTRA_ROWS, :] = table.astype(BF16)
    seeds_copy.wait()


def restart_kernel(me_ref, seeds_ref, out_ref, pick_ref, counts):
    seed_cols = seeds_ref.shape[0]
    tiles = counts.shape[1]
    me = me_ref[0]
    spot = lax.broadcasted_iota(jnp.int32, (tiles, TILE), 0)
    offset = spot // 16
    for place, (z, x) in enumerate(ORDER):
        offset = offset + jnp.where((spot // 2) % 8 == place, 4 * z + 2 * x, 0)
    tile_ids = (me ^ offset) * 2 + spot % 2
    lows = lax.broadcasted_iota(jnp.int32, (TILE, TILE), 0)
    core, x_pos = me % 2, (me // 2) % 2
    pick_row = lax.broadcasted_iota(jnp.int32, pick_ref.shape, 0)
    pick_col = lax.broadcasted_iota(jnp.int32, pick_ref.shape, 1) // TILE
    sib = pick_col // 4
    wanted = 4 * (x_pos ^ ((pick_col // 2) % 2)) + 2 * (core ^ sib) + pick_col % 2
    pick_ref[...] = (pick_row == wanted).astype(F32).astype(BF16)

    @pl.loop(0, seed_cols, unroll=16)
    def _(k):
        row = seeds_ref[pl.ds(k, 1), :]
        high_hot = (tile_ids == row // TILE).astype(F32).astype(BF16)
        low_hot = (lows == row % TILE).astype(F32).astype(BF16)
        counts[k] = dot_nt(high_hot, low_hot) * float(SEED_SHARE)

    for t in range(tiles):
        out_ref[0:seed_cols, t * TILE : (t + 1) * TILE] = counts[:, t, :].astype(BF16)
    rest = out_ref.shape[0] - seed_cols
    first = lax.broadcasted_iota(jnp.int32, (rest, out_ref.shape[1]), 0) == 0
    out_ref[seed_cols:, :] = first.astype(F32).astype(BF16)


def stage_kernel(stage, me_ref, rt_ref, pick_ref, *refs):
    own_names, other_names = OWN_STAGES[stage], OTHER_STAGES[stage]
    count = len(own_names) + len(other_names)
    arrivals, refs = refs[:count], refs[count:]
    if stage > 0:
        refs = refs[4 if stage == len(OWN_STAGES) - 1 else 5 :]
    units, bias, kt_ref, total_ref = refs[:4]
    refs = refs[4:]
    me = me_ref[0]
    z_pos = me // 4
    rows = units.shape[0] // 16
    names = [(0, one) for one in own_names] + [(1, one) for one in other_names]
    for (side, one), ref in zip(names, arrivals):
        place = side * 8 + PLACE[one]
        units[place * rows : (place + 1) * rows] = ref[0:rows]
    if names:
        tables = jnp.concatenate(
            [ref[rows : rows + EXTRA_ROWS, 0:TILE] for ref in arrivals], axis=0
        )
        live = jnp.where(dot_nn(tables, pick_ref[...]) > 0.5, -SLOPE, DEAD)
        for at, (side, (z, x)) in enumerate(names):
            group = (side * 2 + x) * 8
            for xs in range(2):
                lane = PLACE[(z, xs)] * rows
                bias[group : group + 8, lane : lane + rows] = live[
                    at * EXTRA_ROWS : at * EXTRA_ROWS + 8, xs * rows : (xs + 1) * rows
                ]
            if side == 0 and z == 0:
                bias[group : group + 8, 8 * rows : 9 * rows] = live[
                    at * EXTRA_ROWS : at * EXTRA_ROWS + 8, 2 * rows : 3 * rows
                ]
    if stage == 0:
        total_ref[...] = jnp.zeros_like(total_ref)
    tasks = stage_tasks(stage)
    for first, end, spans in tasks:
        lanes = slice(first * rows, end * rows)
        for low, high in spans:
            inner = dot_nt(units[low * rows : high * rows, :], units[lanes, :])
            for tile in range((high - low) * rows // TILE):
                source = low + tile // 2
                z, x = ORDER[source % 8]
                bias_row = (source // 8 * 2 + x) * 8 + 2 * (z_pos ^ z) + tile % 2
                shift = bias[pl.ds(bias_row, 1), lanes]
                value = jnp.exp2(inner[tile * TILE : (tile + 1) * TILE] * SLOPE + shift)
                kt_ref[low * rows + tile * TILE : low * rows + (tile + 1) * TILE, lanes] = value.astype(BF16)
    kept = total_ref.shape[0]
    for first, end, spans in tasks:
        if first == 8:
            continue
        lanes = slice(first * rows, min(end, 8) * rows)
        total = total_ref[:, lanes]
        for low, high in spans:
            sources = slice(low * rows, high * rows)
            total = total + dot_nn(rt_ref[:, sources], kt_ref[sources, lanes])[0:kept]
        total_ref[:, lanes] = total
    if stage < len(OWN_STAGES) - 1:
        refs[0][...] = jnp.zeros_like(refs[0])
        return
    next_ref, gain_ref = refs
    seed_cols = next_ref.shape[0]
    chunk = 512
    for c in range(next_ref.shape[1] // chunk):
        lanes = slice(c * chunk, (c + 1) * chunk)
        gain = DAMPING / total_ref[seed_cols : seed_cols + 8, lanes]
        gain_ref[:, lanes] = gain
        next_ref[:, lanes] = (
            (1.0 - DAMPING) * rt_ref[0:seed_cols, lanes].astype(F32) + total_ref[0:seed_cols, lanes] * gain[0:1]
        ).astype(BF16)


def padded(ranks):
    return jnp.concatenate([ranks, jnp.zeros_like(ranks)], axis=0)


def half_kernel(kt_ref, mine_ref, out_ref):
    seed_cols, own = mine_ref.shape
    mine = padded(mine_ref[...])
    chunk = 512
    for c in range(own // chunk):
        lanes = slice(c * chunk, (c + 1) * chunk)
        out_ref[:, lanes] = dot_nn(mine, kt_ref[0:own, lanes])[0:seed_cols]


def step_kernel(rt_ref, kt_ref, gain_ref, half_ref, other_ref, mine_ref, sent_ref, ranks):
    seed_cols, rows = mine_ref.shape
    own = half_ref.shape[1]
    other = padded(other_ref[...])
    chunk = 512
    for c in range(own // chunk):
        lanes = slice(c * chunk, (c + 1) * chunk)
        total = half_ref[:, lanes] + dot_nn(other, kt_ref[own:, lanes])[0:seed_cols]
        ranks[0:seed_cols, lanes] = (
            (1.0 - DAMPING) * rt_ref[0:seed_cols, lanes].astype(F32) + total * gain_ref[0:1, lanes]
        ).astype(BF16)
    ranks[seed_cols:, :] = jnp.zeros((ranks.shape[0] - seed_cols, own), BF16)
    sent_ref[...] = dot_nn(ranks[...], kt_ref[0:own, own : own + rows])[0:seed_cols]
    mine_ref[...] = dot_nn(ranks[...], kt_ref[0:own, 0:rows])[0:seed_cols]


def last_kernel(rt_ref, gain_ref, mine_ref, other_ref, out_ref):
    seed_cols, rows = out_ref.shape
    total = mine_ref[...] + other_ref[...]
    out_ref[...] = (1.0 - DAMPING) * rt_ref[0:seed_cols, 0:rows].astype(F32) + total * gain_ref[0:1, 0:rows]


WHOLE = pl.BlockSpec(memory_space=pltpu.VMEM)
SCALARS = pl.BlockSpec(memory_space=pltpu.SMEM)
REMAIN = pl.BlockSpec(memory_space=pl.ANY)


def params():
    return pltpu.CompilerParams(vmem_limit_bytes=20 * 2**20)


def in_hbm(array):
    return pltpu.with_memory_space_constraint(array, pltpu.HBM)


def work(micros):
    return pl.CostEstimate(flops=int(micros * 1000), bytes_accessed=int(micros * 100), transcendentals=0)


def swap(array, mapping):
    pairs = [(device, mapping(device)) for device in range(16)]
    return lax.ppermute(array, ("row", "col"), pairs)


def near(device):
    return device ^ 4


def far(device):
    return device ^ 8


def across(device):
    return device ^ 2


def diagonal(device):
    return device ^ 6


def sibling(device):
    return device ^ 1


def chip_local(embeddings, tile_list, tile_count, seeds):
    row_pos = lax.axis_index("row")
    me = (row_pos * 4 + lax.axis_index("col")).reshape(1)
    rows, width = embeddings.shape
    seed_cols = seeds.shape[0]
    sessions = rows * 16
    own = rows * 8
    slots = tile_list.shape[3]
    block, seeds = pl.pallas_call(
        payload_kernel,
        in_specs=[SCALARS] + [REMAIN] * 3,
        out_specs=[WHOLE] * 2,
        out_shape=[
            pltpu.VMEM((rows + EXTRA_ROWS, width), BF16),
            pltpu.VMEM(seeds.shape, seeds.dtype),
        ],
        scratch_shapes=[
            pltpu.VMEM((rows, width), BF16),
            pltpu.VMEM((2, slots), jnp.int32),
            pltpu.SemaphoreType.DMA((3,)),
        ],
        compiler_params=params(),
        name="payload",
    )(tile_count, in_hbm(embeddings), in_hbm(tile_list.reshape(2, slots)), in_hbm(seeds))
    state_shapes = [
        pltpu.VMEM((sessions, width), BF16),
        pltpu.VMEM((32, own + rows), F32),
        pltpu.VMEM((sessions, own + rows), BF16),
        pltpu.VMEM((seed_cols + 8, own), F32),
    ]
    mark = [jax.ShapeDtypeStruct((8, TILE), F32)]

    def run_stage(stage, rt, arrivals, state, extra, *after):
        first_state = 3 + len(arrivals)
        outs = pl.pallas_call(
            functools.partial(stage_kernel, stage),
            in_specs=[SCALARS] + [WHOLE] * (2 + len(arrivals) + len(state)) + [REMAIN] * len(after),
            out_specs=[WHOLE] * (4 + len(extra)),
            out_shape=state_shapes + extra,
            input_output_aliases={first_state + k: k for k in range(len(state))},
            compiler_params=params(),
            cost_estimate=work(2.5),
            name=f"stage{stage}",
        )(me, rt, pick, *arrivals, *state, *after)
        return outs[:4], outs[4:]

    z1 = swap(block, near)
    z2 = swap(block, far)
    x0 = swap(block, across)
    b00 = swap(block, sibling)
    rt, pick = pl.pallas_call(
        restart_kernel,
        in_specs=[SCALARS, WHOLE],
        out_specs=[WHOLE] * 2,
        out_shape=[
            jax.ShapeDtypeStruct((2 * seed_cols, sessions), BF16),
            jax.ShapeDtypeStruct((TILE, 6 * TILE), BF16),
        ],
        scratch_shapes=[pltpu.VMEM((seed_cols, sessions // TILE, TILE), F32)],
        compiler_params=params(),
        cost_estimate=work(2.6),
        name="restart",
    )(me, seeds)
    z1, x0, rt = lax.optimization_barrier((z1, x0, rt))
    x1 = swap(z1, across)
    b10 = swap(z1, sibling)
    b01 = swap(x0, sibling)
    state, (done,) = run_stage(0, rt, [block, z1, x0], [], mark)
    z2, b00, done = lax.optimization_barrier((z2, b00, done))
    z3 = swap(z2, near)
    x2 = swap(z2, across)
    x3 = swap(z2, diagonal)
    state, (done,) = run_stage(1, rt, [z2, x1, b00, b10, b01], state, mark, done)
    z2, x1, done = lax.optimization_barrier((z2, x1, done))
    b20 = swap(z2, sibling)
    b11 = swap(x1, sibling)
    x2, z3, done = lax.optimization_barrier((x2, z3, done))
    state, (done,) = run_stage(2, rt, [z3, x2], state, mark, done)
    x2, z3, done = lax.optimization_barrier((x2, z3, done))
    b30 = swap(z3, sibling)
    b21 = swap(x2, sibling)
    b31 = swap(x3, sibling)
    state, (done,) = run_stage(3, rt, [x3, b20, b11], state, mark, done)
    state, (ranks, gain) = run_stage(
        4,
        rt,
        [b30, b21, b31],
        state,
        [jax.ShapeDtypeStruct((seed_cols, own), BF16), jax.ShapeDtypeStruct((8, own), F32)],
    )
    kt = state[2]
    half = pl.pallas_call(
        half_kernel,
        in_specs=[WHOLE] * 2,
        out_specs=WHOLE,
        out_shape=jax.ShapeDtypeStruct((seed_cols, own), F32),
        compiler_params=params(),
        cost_estimate=work(1.5),
        name="half",
    )(kt, ranks)
    mine, sent = pl.pallas_call(
        step_kernel,
        in_specs=[WHOLE] * 5,
        out_specs=[WHOLE] * 2,
        out_shape=[jax.ShapeDtypeStruct((seed_cols, rows), F32)] * 2,
        scratch_shapes=[pltpu.VMEM((2 * seed_cols, own), BF16)],
        compiler_params=params(),
        cost_estimate=work(1.5),
        name="step",
    )(rt, kt, gain, half, swap(ranks, sibling))
    result = pl.pallas_call(
        last_kernel,
        in_specs=[WHOLE] * 4,
        out_specs=WHOLE,
        out_shape=jax.ShapeDtypeStruct((seed_cols, rows), F32),
        compiler_params=params(),
        cost_estimate=work(0.5),
        name="last",
    )(rt, gain, mine, swap(sent, sibling))
    return result.T


def block_width():
    for option_width in (16, 8, 4, 2):
        return option_width
    return 1


def seed_mass(seed_index, is_valid, length):
    spots = jnp.arange(length, dtype=jnp.int32)

    def one_column(pieces):
        index_row, valid_row = pieces
        hits = (index_row[:, None] == spots[None, :]) & valid_row[:, None]
        return jnp.sum(hits.astype(jnp.float32), axis=0) * float(SEED_SHARE)

    table = lax.map(one_column, (seed_index, is_valid))
    return table.T


def grid_local(embeddings, tile_list, tile_count, seeds):
    n_row = lax.axis_size("row")
    n_col = lax.axis_size("col")
    row_pos = lax.axis_index("row")
    col_pos = lax.axis_index("col")
    slice_rows = embeddings.shape[0]
    grid_rows = slice_rows * n_col
    row_tiles = grid_rows // TILE
    col_tiles = slice_rows * n_row // TILE
    seed_cols = seeds.shape[0]
    unit_rows = normalize(embeddings)
    row_emb = lax.all_gather(unit_rows, "col", axis=0, tiled=True).reshape(row_tiles, TILE, -1)
    col_emb = lax.all_gather(unit_rows, "row", axis=0, tiled=True).reshape(col_tiles, TILE, -1)
    slots = tile_list.shape[3]
    width_b = block_width()
    turn_count = slots // width_b
    row_ids = tile_list[0, 0, 0]
    col_ids = tile_list[0, 0, 1]
    live_mask = (jnp.arange(slots, dtype=jnp.int32) < tile_count[0, 0]).astype(jnp.float32)
    row_blocks = row_ids.reshape(turn_count, width_b)
    col_blocks = col_ids.reshape(turn_count, width_b)
    live_blocks = live_mask.reshape(turn_count, width_b)

    def kernel_turn(degree, pieces):
        row_part, col_part, live_part = pieces
        left_tiles = jnp.take(row_emb, row_part, axis=0)
        right_tiles = jnp.take(col_emb, col_part, axis=0)
        inner_prod = jnp.einsum(
            "bie,bje->bij", left_tiles, right_tiles, preferred_element_type=jnp.float32
        )
        values = jnp.exp(KERNEL_GAIN * (2.0 * inner_prod - 2.0)).astype(jnp.bfloat16)
        row_total = jnp.sum(values.astype(jnp.float32), axis=2)
        degree = degree.at[row_part].add(row_total * live_part[:, None])
        return (degree, values)

    degree_part, kernel = lax.scan(
        kernel_turn,
        jnp.zeros((row_tiles, TILE), jnp.float32),
        (row_blocks, col_blocks, live_blocks),
    )
    degree_part = degree_part.reshape(grid_rows)

    def spread(ranks_col):
        col_ranks = ranks_col.reshape(col_tiles, TILE, seed_cols)

        def rank_turn(running, pieces):
            row_part, col_part, live_part, values = pieces
            right_tiles = jnp.take(col_ranks, col_part, axis=0)
            product = jnp.einsum(
                "bij,bjk->bik", values, right_tiles, preferred_element_type=jnp.float32
            )
            running = running.at[row_part].add(product * live_part[:, None, None])
            return (running, None)

        running, unused = lax.scan(
            rank_turn,
            jnp.zeros((row_tiles, TILE, seed_cols), jnp.float32),
            (row_blocks, col_blocks, live_blocks, kernel),
        )
        return running.reshape(grid_rows, seed_cols)

    own_start = (row_pos * n_col + col_pos) * slice_rows
    own_index = seeds - own_start
    seed_own = seed_mass(own_index, (own_index >= 0) & (own_index < slice_rows), slice_rows)
    degree = lax.psum_scatter(degree_part, "col", scatter_dimension=0, tiled=True)
    opening = lax.all_gather(seed_own.astype(jnp.bfloat16), "row", axis=0, tiled=True)
    partial_rows = spread(opening)
    summed = lax.psum_scatter(partial_rows, "col", scatter_dimension=0, tiled=True)
    rank_rows = (1.0 - DAMPING) * seed_own + DAMPING * summed / degree[:, None]
    for sweep_idx in range(ITERS - 1):
        gathered = lax.all_gather(rank_rows.astype(jnp.bfloat16), "row", axis=0, tiled=True)
        partial_rows = spread(gathered)
        summed = lax.psum_scatter(partial_rows, "col", scatter_dimension=0, tiled=True)
        rank_rows = (1.0 - DAMPING) * seed_own + DAMPING * summed / degree[:, None]
    return rank_rows


def solution(mesh):
    n_row, n_col = mesh.shape["row"], mesh.shape["col"]

    def local(embeddings, tile_list, tile_count, seeds):
        small = n_row == 4 and n_col == 4 and embeddings.shape == (2 * TILE, 2 * TILE)
        if small and seeds.shape == (64, TILE):
            return chip_local(embeddings, tile_list, tile_count, seeds)
        return grid_local(embeddings, tile_list, tile_count, seeds)

    return jax.shard_map(
        local,
        mesh=mesh,
        in_specs=(
            P(("groups", "row", "col"), None),
            P(("groups", "row"), "col", None, None),
            P(("groups", "row"), "col"),
            P("groups", None),
        ),
        out_specs=P(("groups", "row", "col"), None),
        check_vma=False,
    )
```

```python
import functools
import math

import jax
import jax.numpy as jnp
from jax import lax
from jax.experimental import pallas as pl
from jax.experimental.pallas import tpu as pltpu
from jax.sharding import PartitionSpec as P

TILE = 128
ITERS = 3
SEED_SHARE = 32


KERNEL_GAIN = 4.0
DAMPING = 0.85
EPSILON = 1e-06

SLOPE = 2.0 * KERNEL_GAIN * math.log2(math.e)
DEAD = -1e9
MASK_ROWS = 16
EXTRA_ROWS = 16

F32 = jnp.float32
BF16 = jnp.bfloat16


def normalize(rows_in):
    widened = rows_in.astype(F32)
    factor = lax.rsqrt(jnp.mean(widened * widened, axis=-1, keepdims=True) + EPSILON)
    return (widened * factor * widened.shape[-1] ** (-0.5)).astype(BF16)


ORDER = ((0, 0), (0, 1), (1, 1), (1, 0), (2, 0), (2, 1), (3, 0), (3, 1))
PLACE = {block: place for place, block in enumerate(ORDER)}
OWN_STAGES = (
    ((0, 0), (1, 0), (0, 1)),
    ((2, 0),),
    ((1, 1),),
    ((3, 0), (2, 1)),
    ((3, 1),),
    (),
)
OTHER_STAGES = (
    (),
    ((0, 0),),
    ((1, 0), (0, 1)),
    ((2, 0), (1, 1)),
    ((3, 0), (2, 1)),
    ((3, 1),),
)


def runs_of(places):
    found = []
    for place in sorted(places):
        if found and found[-1][1] == place:
            found[-1][1] = place + 1
        else:
            found.append([place, place + 1])
    return found


def stage_tasks(stage):
    here, before = set(), set()
    for at_stage in range(stage + 1):
        before = set(here)
        blocks = [set(sum(names[: at_stage + 1], ())) for names in (OWN_STAGES, OTHER_STAGES)]
        for target in blocks[0]:
            for side in (0, 1):
                for source in blocks[side]:
                    if (target[0], source[1]) in blocks[side]:
                        here.add((PLACE[target], side * 8 + PLACE[source]))
        if (0, 0) in blocks[1]:
            here.update((8, PLACE[source]) for source in blocks[0] if (0, source[1]) in blocks[0])
    wanted = {}
    for target, source in here - before:
        wanted.setdefault(target, set()).add(source)
    tasks = []
    for sources in sorted({tuple(sorted(one)) for one in wanted.values()}):
        for low, high in runs_of([target for target in wanted if tuple(sorted(wanted[target])) == sources]):
            tasks.append((low, high, runs_of(sources)))
    return tasks


def dot_nt(lhs, rhs):
    return lax.dot_general(lhs, rhs, (((1,), (1,)), ((), ())), preferred_element_type=F32)


def dot_nn(lhs, rhs):
    return lax.dot_general(lhs, rhs, (((1,), (0,)), ((), ())), preferred_element_type=F32)


def payload_kernel(count_ref, emb_in, list_in, seeds_in, out_ref, seeds_ref, emb_ref, list_ref, sems):
    rows = emb_ref.shape[0]
    width = emb_ref.shape[1]
    slots = list_ref.shape[1]
    emb_copy = pltpu.make_async_copy(emb_in, emb_ref, sems.at[0])
    list_copy = pltpu.make_async_copy(list_in, list_ref, sems.at[1])
    seeds_copy = pltpu.make_async_copy(seeds_in, seeds_ref, sems.at[2])
    emb_copy.start()
    list_copy.start()
    seeds_copy.start()
    emb_copy.wait()
    list_copy.wait()
    out_ref[0:rows, :] = normalize(emb_ref[...])
    live = lax.broadcasted_iota(jnp.int32, (1, slots), 1) < count_ref[0, 0]
    col_hot = (lax.broadcasted_iota(jnp.int32, (EXTRA_ROWS, slots), 0) == list_ref[1:2, :]) & live
    row_hot = lax.broadcasted_iota(jnp.int32, (width, slots), 0) == list_ref[0:1, :]
    table = dot_nt(col_hot.astype(F32).astype(BF16), row_hot.astype(F32).astype(BF16))
    out_ref[rows : rows + EXTRA_ROWS, :] = table.astype(BF16)
    seeds_copy.wait()


def restart_kernel(me_ref, seeds_ref, out_ref, pick_ref, counts):
    seed_cols = seeds_ref.shape[0]
    tiles = counts.shape[1]
    me = me_ref[0]
    spot = lax.broadcasted_iota(jnp.int32, (tiles, TILE), 0)
    offset = spot // 16
    for place, (z, x) in enumerate(ORDER):
        offset = offset + jnp.where((spot // 2) % 8 == place, 4 * z + 2 * x, 0)
    tile_ids = (me ^ offset) * 2 + spot % 2
    lows = lax.broadcasted_iota(jnp.int32, (TILE, TILE), 0)
    core, x_pos = me % 2, (me // 2) % 2
    pick_row = lax.broadcasted_iota(jnp.int32, pick_ref.shape, 0)
    pick_col = lax.broadcasted_iota(jnp.int32, pick_ref.shape, 1) // TILE
    sib = pick_col // 4
    wanted = 4 * (x_pos ^ ((pick_col // 2) % 2)) + 2 * (core ^ sib) + pick_col % 2
    pick_ref[...] = (pick_row == wanted).astype(F32).astype(BF16)

    @pl.loop(0, seed_cols, unroll=16)
    def _(k):
        row = seeds_ref[pl.ds(k, 1), :]
        high_hot = (tile_ids == row // TILE).astype(F32).astype(BF16)
        low_hot = (lows == row % TILE).astype(F32).astype(BF16)
        counts[k] = dot_nt(high_hot, low_hot) * float(SEED_SHARE)

    for t in range(tiles):
        out_ref[0:seed_cols, t * TILE : (t + 1) * TILE] = counts[:, t, :].astype(BF16)
    rest = out_ref.shape[0] - seed_cols
    first = lax.broadcasted_iota(jnp.int32, (rest, out_ref.shape[1]), 0) == 0
    out_ref[seed_cols:, :] = first.astype(F32).astype(BF16)


def stage_kernel(stage, me_ref, rt_ref, pick_ref, *refs):
    own_names, other_names = OWN_STAGES[stage], OTHER_STAGES[stage]
    count = len(own_names) + len(other_names)
    arrivals, refs = refs[:count], refs[count:]
    if stage > 0:
        refs = refs[4 if stage == len(OWN_STAGES) - 1 else 5 :]
    units, bias, kt_ref, total_ref = refs[:4]
    refs = refs[4:]
    me = me_ref[0]
    z_pos = me // 4
    rows = units.shape[0] // 16
    names = [(0, one) for one in own_names] + [(1, one) for one in other_names]
    for (side, one), ref in zip(names, arrivals):
        place = side * 8 + PLACE[one]
        units[place * rows : (place + 1) * rows] = ref[0:rows]
    if names:
        tables = jnp.concatenate(
            [ref[rows : rows + EXTRA_ROWS, 0:TILE] for ref in arrivals], axis=0
        )
        live = jnp.where(dot_nn(tables, pick_ref[...]) > 0.5, -SLOPE, DEAD)
        for at, (side, (z, x)) in enumerate(names):
            group = (side * 2 + x) * 8
            for xs in range(2):
                lane = PLACE[(z, xs)] * rows
                bias[group : group + 8, lane : lane + rows] = live[
                    at * EXTRA_ROWS : at * EXTRA_ROWS + 8, xs * rows : (xs + 1) * rows
                ]
            if side == 0 and z == 0:
                bias[group : group + 8, 8 * rows : 9 * rows] = live[
                    at * EXTRA_ROWS : at * EXTRA_ROWS + 8, 2 * rows : 3 * rows
                ]
    if stage == 0:
        total_ref[...] = jnp.zeros_like(total_ref)
    tasks = stage_tasks(stage)
    for first, end, spans in tasks:
        lanes = slice(first * rows, end * rows)
        for low, high in spans:
            inner = dot_nt(units[low * rows : high * rows, :], units[lanes, :])
            for tile in range((high - low) * rows // TILE):
                source = low + tile // 2
                z, x = ORDER[source % 8]
                bias_row = (source // 8 * 2 + x) * 8 + 2 * (z_pos ^ z) + tile % 2
                shift = bias[pl.ds(bias_row, 1), lanes]
                value = jnp.exp2(inner[tile * TILE : (tile + 1) * TILE] * SLOPE + shift)
                kt_ref[low * rows + tile * TILE : low * rows + (tile + 1) * TILE, lanes] = value.astype(BF16)
    kept = total_ref.shape[0]
    for first, end, spans in tasks:
        if first == 8:
            continue
        lanes = slice(first * rows, min(end, 8) * rows)
        scores = jnp.concatenate([rt_ref[:, low * rows : high * rows] for low, high in spans], axis=1)
        values = jnp.concatenate([kt_ref[low * rows : high * rows, lanes] for low, high in spans], axis=0)
        total_ref[:, lanes] = total_ref[:, lanes] + dot_nn(scores, values)[0:kept]
    if stage < len(OWN_STAGES) - 1:
        if refs:
            refs[0][...] = jnp.zeros_like(refs[0])
        return
    next_ref, gain_ref = refs
    seed_cols = next_ref.shape[0]
    chunk = 512
    for c in range(next_ref.shape[1] // chunk):
        lanes = slice(c * chunk, (c + 1) * chunk)
        gain = DAMPING / total_ref[seed_cols : seed_cols + 8, lanes]
        gain_ref[:, lanes] = gain
        next_ref[:, lanes] = (
            (1.0 - DAMPING) * rt_ref[0:seed_cols, lanes].astype(F32) + total_ref[0:seed_cols, lanes] * gain[0:1]
        ).astype(BF16)


def padded(ranks):
    return jnp.concatenate([ranks, jnp.zeros_like(ranks)], axis=0)


def half_kernel(kt_ref, mine_ref, out_ref):
    seed_cols, own = mine_ref.shape
    mine = padded(mine_ref[...])
    chunk = 512
    for c in range(own // chunk):
        lanes = slice(c * chunk, (c + 1) * chunk)
        out_ref[:, lanes] = dot_nn(mine, kt_ref[0:own, lanes])[0:seed_cols]


def step_kernel(rt_ref, kt_ref, gain_ref, half_ref, other_ref, mine_ref, sent_ref, ranks):
    seed_cols, rows = mine_ref.shape
    own = half_ref.shape[1]
    other = padded(other_ref[...])
    chunk = 512
    for c in range(own // chunk):
        lanes = slice(c * chunk, (c + 1) * chunk)
        total = half_ref[:, lanes] + dot_nn(other, kt_ref[own:, lanes])[0:seed_cols]
        ranks[0:seed_cols, lanes] = (
            (1.0 - DAMPING) * rt_ref[0:seed_cols, lanes].astype(F32) + total * gain_ref[0:1, lanes]
        ).astype(BF16)
    ranks[seed_cols:, :] = jnp.zeros((ranks.shape[0] - seed_cols, own), BF16)
    sent_ref[...] = dot_nn(ranks[...], kt_ref[0:own, own : own + rows])[0:seed_cols]
    mine_ref[...] = dot_nn(ranks[...], kt_ref[0:own, 0:rows])[0:seed_cols]


def last_kernel(rt_ref, gain_ref, mine_ref, other_ref, out_ref):
    seed_cols, rows = out_ref.shape
    total = mine_ref[...] + other_ref[...]
    out_ref[...] = (1.0 - DAMPING) * rt_ref[0:seed_cols, 0:rows].astype(F32) + total * gain_ref[0:1, 0:rows]


WHOLE = pl.BlockSpec(memory_space=pltpu.VMEM)
SCALARS = pl.BlockSpec(memory_space=pltpu.SMEM)
REMAIN = pl.BlockSpec(memory_space=pl.ANY)


def params():
    return pltpu.CompilerParams(vmem_limit_bytes=20 * 2**20)


def in_hbm(array):
    return pltpu.with_memory_space_constraint(array, pltpu.HBM)


def work(micros):
    return pl.CostEstimate(flops=int(micros * 1000), bytes_accessed=int(micros * 100), transcendentals=0)


def swap(array, mapping):
    pairs = [(device, mapping(device)) for device in range(16)]
    return lax.ppermute(array, ("row", "col"), pairs)


def near(device):
    return device ^ 4


def far(device):
    return device ^ 8


def across(device):
    return device ^ 2


def diagonal(device):
    return device ^ 6


def sibling(device):
    return device ^ 1


def chip_local(embeddings, tile_list, tile_count, seeds):
    row_pos = lax.axis_index("row")
    me = (row_pos * 4 + lax.axis_index("col")).reshape(1)
    rows, width = embeddings.shape
    seed_cols = seeds.shape[0]
    sessions = rows * 16
    own = rows * 8
    slots = tile_list.shape[3]
    block, seeds = pl.pallas_call(
        payload_kernel,
        in_specs=[SCALARS] + [REMAIN] * 3,
        out_specs=[WHOLE] * 2,
        out_shape=[
            pltpu.VMEM((rows + EXTRA_ROWS, width), BF16),
            pltpu.VMEM(seeds.shape, seeds.dtype),
        ],
        scratch_shapes=[
            pltpu.VMEM((rows, width), BF16),
            pltpu.VMEM((2, slots), jnp.int32),
            pltpu.SemaphoreType.DMA((3,)),
        ],
        compiler_params=params(),
        name="payload",
    )(tile_count, in_hbm(embeddings), in_hbm(tile_list.reshape(2, slots)), in_hbm(seeds))
    state_shapes = [
        pltpu.VMEM((sessions, width), BF16),
        pltpu.VMEM((32, own + rows), F32),
        pltpu.VMEM((sessions, own + rows), BF16),
        pltpu.VMEM((seed_cols + 8, own), F32),
    ]
    mark = [jax.ShapeDtypeStruct((8, TILE), F32)]

    def run_stage(stage, rt, arrivals, state, extra, *after):
        first_state = 3 + len(arrivals)
        outs = pl.pallas_call(
            functools.partial(stage_kernel, stage),
            in_specs=[SCALARS] + [WHOLE] * (2 + len(arrivals) + len(state)) + [REMAIN] * len(after),
            out_specs=[WHOLE] * (4 + len(extra)),
            out_shape=state_shapes + extra,
            input_output_aliases={first_state + k: k for k in range(len(state))},
            compiler_params=params(),
            cost_estimate=work(2.5),
            name=f"stage{stage}",
        )(me, rt, pick, *arrivals, *state, *after)
        return outs[:4], outs[4:]

    z1 = swap(block, near)
    z2 = swap(block, far)
    x0 = swap(block, across)
    b00 = swap(block, sibling)
    rt, pick = pl.pallas_call(
        restart_kernel,
        in_specs=[SCALARS, WHOLE],
        out_specs=[WHOLE] * 2,
        out_shape=[
            jax.ShapeDtypeStruct((2 * seed_cols, sessions), BF16),
            jax.ShapeDtypeStruct((TILE, 6 * TILE), BF16),
        ],
        scratch_shapes=[pltpu.VMEM((seed_cols, sessions // TILE, TILE), F32)],
        compiler_params=params(),
        cost_estimate=work(2.6),
        name="restart",
    )(me, seeds)
    z1, x0, rt = lax.optimization_barrier((z1, x0, rt))
    x1 = swap(z1, across)
    b10 = swap(z1, sibling)
    b01 = swap(x0, sibling)
    state, (done,) = run_stage(0, rt, [block, z1, x0], [], mark)
    z2, b00, done = lax.optimization_barrier((z2, b00, done))
    z3 = swap(z2, near)
    x2 = swap(z2, across)
    state, (done,) = run_stage(1, rt, [z2, b00], state, mark, done)
    z2, done = lax.optimization_barrier((z2, done))
    x3 = swap(z2, diagonal)
    b20 = swap(z2, sibling)
    b11 = swap(x1, sibling)
    state, (done,) = run_stage(2, rt, [x1, b10, b01], state, mark, done)
    x2, z3, done = lax.optimization_barrier((x2, z3, done))
    b30 = swap(z3, sibling)
    b21 = swap(x2, sibling)
    state, (done,) = run_stage(3, rt, [z3, x2, b20, b11], state, mark, done)
    x3, done = lax.optimization_barrier((x3, done))
    b31 = swap(x3, sibling)
    state, _ = run_stage(4, rt, [x3, b30, b21], state, [], done)
    state, (ranks, gain) = run_stage(
        5,
        rt,
        [b31],
        state,
        [jax.ShapeDtypeStruct((seed_cols, own), BF16), jax.ShapeDtypeStruct((8, own), F32)],
    )
    kt = state[2]
    half = pl.pallas_call(
        half_kernel,
        in_specs=[WHOLE] * 2,
        out_specs=WHOLE,
        out_shape=jax.ShapeDtypeStruct((seed_cols, own), F32),
        compiler_params=params(),
        cost_estimate=work(1.5),
        name="half",
    )(kt, ranks)
    mine, sent = pl.pallas_call(
        step_kernel,
        in_specs=[WHOLE] * 5,
        out_specs=[WHOLE] * 2,
        out_shape=[jax.ShapeDtypeStruct((seed_cols, rows), F32)] * 2,
        scratch_shapes=[pltpu.VMEM((2 * seed_cols, own), BF16)],
        compiler_params=params(),
        cost_estimate=work(1.5),
        name="step",
    )(rt, kt, gain, half, swap(ranks, sibling))
    result = pl.pallas_call(
        last_kernel,
        in_specs=[WHOLE] * 4,
        out_specs=WHOLE,
        out_shape=jax.ShapeDtypeStruct((seed_cols, rows), F32),
        compiler_params=params(),
        cost_estimate=work(0.5),
        name="last",
    )(rt, gain, mine, swap(sent, sibling))
    return result.T


def block_width():
    for option_width in (16, 8, 4, 2):
        return option_width
    return 1


def seed_mass(seed_index, is_valid, length):
    spots = jnp.arange(length, dtype=jnp.int32)

    def one_column(pieces):
        index_row, valid_row = pieces
        hits = (index_row[:, None] == spots[None, :]) & valid_row[:, None]
        return jnp.sum(hits.astype(jnp.float32), axis=0) * float(SEED_SHARE)

    table = lax.map(one_column, (seed_index, is_valid))
    return table.T


def grid_local(embeddings, tile_list, tile_count, seeds):
    n_row = lax.axis_size("row")
    n_col = lax.axis_size("col")
    row_pos = lax.axis_index("row")
    col_pos = lax.axis_index("col")
    slice_rows = embeddings.shape[0]
    grid_rows = slice_rows * n_col
    row_tiles = grid_rows // TILE
    col_tiles = slice_rows * n_row // TILE
    seed_cols = seeds.shape[0]
    unit_rows = normalize(embeddings)
    row_emb = lax.all_gather(unit_rows, "col", axis=0, tiled=True).reshape(row_tiles, TILE, -1)
    col_emb = lax.all_gather(unit_rows, "row", axis=0, tiled=True).reshape(col_tiles, TILE, -1)
    slots = tile_list.shape[3]
    width_b = block_width()
    turn_count = slots // width_b
    row_ids = tile_list[0, 0, 0]
    col_ids = tile_list[0, 0, 1]
    live_mask = (jnp.arange(slots, dtype=jnp.int32) < tile_count[0, 0]).astype(jnp.float32)
    row_blocks = row_ids.reshape(turn_count, width_b)
    col_blocks = col_ids.reshape(turn_count, width_b)
    live_blocks = live_mask.reshape(turn_count, width_b)

    def kernel_turn(degree, pieces):
        row_part, col_part, live_part = pieces
        left_tiles = jnp.take(row_emb, row_part, axis=0)
        right_tiles = jnp.take(col_emb, col_part, axis=0)
        inner_prod = jnp.einsum(
            "bie,bje->bij", left_tiles, right_tiles, preferred_element_type=jnp.float32
        )
        values = jnp.exp(KERNEL_GAIN * (2.0 * inner_prod - 2.0)).astype(jnp.bfloat16)
        row_total = jnp.sum(values.astype(jnp.float32), axis=2)
        degree = degree.at[row_part].add(row_total * live_part[:, None])
        return (degree, values)

    degree_part, kernel = lax.scan(
        kernel_turn,
        jnp.zeros((row_tiles, TILE), jnp.float32),
        (row_blocks, col_blocks, live_blocks),
    )
    degree_part = degree_part.reshape(grid_rows)

    def spread(ranks_col):
        col_ranks = ranks_col.reshape(col_tiles, TILE, seed_cols)

        def rank_turn(running, pieces):
            row_part, col_part, live_part, values = pieces
            right_tiles = jnp.take(col_ranks, col_part, axis=0)
            product = jnp.einsum(
                "bij,bjk->bik", values, right_tiles, preferred_element_type=jnp.float32
            )
            running = running.at[row_part].add(product * live_part[:, None, None])
            return (running, None)

        running, unused = lax.scan(
            rank_turn,
            jnp.zeros((row_tiles, TILE, seed_cols), jnp.float32),
            (row_blocks, col_blocks, live_blocks, kernel),
        )
        return running.reshape(grid_rows, seed_cols)

    own_start = (row_pos * n_col + col_pos) * slice_rows
    own_index = seeds - own_start
    seed_own = seed_mass(own_index, (own_index >= 0) & (own_index < slice_rows), slice_rows)
    degree = lax.psum_scatter(degree_part, "col", scatter_dimension=0, tiled=True)
    opening = lax.all_gather(seed_own.astype(jnp.bfloat16), "row", axis=0, tiled=True)
    partial_rows = spread(opening)
    summed = lax.psum_scatter(partial_rows, "col", scatter_dimension=0, tiled=True)
    rank_rows = (1.0 - DAMPING) * seed_own + DAMPING * summed / degree[:, None]
    for sweep_idx in range(ITERS - 1):
        gathered = lax.all_gather(rank_rows.astype(jnp.bfloat16), "row", axis=0, tiled=True)
        partial_rows = spread(gathered)
        summed = lax.psum_scatter(partial_rows, "col", scatter_dimension=0, tiled=True)
        rank_rows = (1.0 - DAMPING) * seed_own + DAMPING * summed / degree[:, None]
    return rank_rows


def solution(mesh):
    n_row, n_col = mesh.shape["row"], mesh.shape["col"]

    def local(embeddings, tile_list, tile_count, seeds):
        small = n_row == 4 and n_col == 4 and embeddings.shape == (2 * TILE, 2 * TILE)
        if small and seeds.shape == (64, TILE):
            return chip_local(embeddings, tile_list, tile_count, seeds)
        return grid_local(embeddings, tile_list, tile_count, seeds)

    return jax.shard_map(
        local,
        mesh=mesh,
        in_specs=(
            P(("groups", "row", "col"), None),
            P(("groups", "row"), "col", None, None),
            P(("groups", "row"), "col"),
            P("groups", None),
        ),
        out_specs=P(("groups", "row", "col"), None),
        check_vma=False,
    )
```

```python
import functools
import math

import jax
import jax.numpy as jnp
from jax import lax
from jax.experimental import pallas as pl
from jax.experimental.pallas import tpu as pltpu
from jax.sharding import PartitionSpec as P

TILE = 128
ITERS = 3
SEED_SHARE = 32


KERNEL_GAIN = 4.0
DAMPING = 0.85
EPSILON = 1e-06

SLOPE = 2.0 * KERNEL_GAIN * math.log2(math.e)
DEAD = -1e9
MASK_ROWS = 16
EXTRA_ROWS = 16

F32 = jnp.float32
BF16 = jnp.bfloat16


def normalize(rows_in):
    widened = rows_in.astype(F32)
    factor = lax.rsqrt(jnp.mean(widened * widened, axis=-1, keepdims=True) + EPSILON)
    return (widened * factor * widened.shape[-1] ** (-0.5)).astype(BF16)


ORDER = ((0, 0), (0, 1), (1, 1), (1, 0), (2, 0), (2, 1), (3, 0), (3, 1))
PLACE = {block: place for place, block in enumerate(ORDER)}
OWN_STAGES = (
    ((0, 0), (1, 0), (0, 1)),
    ((2, 0),),
    ((1, 1),),
    ((3, 0), (2, 1)),
    ((3, 1),),
    (),
)
OTHER_STAGES = (
    (),
    ((0, 0),),
    ((1, 0), (0, 1)),
    ((2, 0), (1, 1)),
    ((3, 0), (2, 1)),
    ((3, 1),),
)


def runs_of(places):
    found = []
    for place in sorted(places):
        if found and found[-1][1] == place:
            found[-1][1] = place + 1
        else:
            found.append([place, place + 1])
    return found


def stage_tasks(stage):
    here, before = set(), set()
    for at_stage in range(stage + 1):
        before = set(here)
        blocks = [set(sum(names[: at_stage + 1], ())) for names in (OWN_STAGES, OTHER_STAGES)]
        for target in blocks[0]:
            for side in (0, 1):
                for source in blocks[side]:
                    if (target[0], source[1]) in blocks[side]:
                        here.add((PLACE[target], side * 8 + PLACE[source]))
        if (0, 0) in blocks[1]:
            here.update((8, PLACE[source]) for source in blocks[0] if (0, source[1]) in blocks[0])
    wanted = {}
    for target, source in here - before:
        wanted.setdefault(target, set()).add(source)
    tasks = []
    for sources in sorted({tuple(sorted(one)) for one in wanted.values()}):
        for low, high in runs_of([target for target in wanted if tuple(sorted(wanted[target])) == sources]):
            tasks.append((low, high, runs_of(sources)))
    return tasks


def dot_nt(lhs, rhs):
    return lax.dot_general(lhs, rhs, (((1,), (1,)), ((), ())), preferred_element_type=F32)


def dot_nn(lhs, rhs):
    return lax.dot_general(lhs, rhs, (((1,), (0,)), ((), ())), preferred_element_type=F32)


def payload_kernel(count_ref, emb_in, list_in, seeds_in, out_ref, seeds_ref, emb_ref, list_ref, sems):
    rows = emb_ref.shape[0]
    width = emb_ref.shape[1]
    slots = list_ref.shape[1]
    emb_copy = pltpu.make_async_copy(emb_in, emb_ref, sems.at[0])
    list_copy = pltpu.make_async_copy(list_in, list_ref, sems.at[1])
    seeds_copy = pltpu.make_async_copy(seeds_in, seeds_ref, sems.at[2])
    emb_copy.start()
    list_copy.start()
    seeds_copy.start()
    emb_copy.wait()
    list_copy.wait()
    out_ref[0:rows, :] = normalize(emb_ref[...])
    live = lax.broadcasted_iota(jnp.int32, (1, slots), 1) < count_ref[0, 0]
    col_hot = (lax.broadcasted_iota(jnp.int32, (EXTRA_ROWS, slots), 0) == list_ref[1:2, :]) & live
    row_hot = lax.broadcasted_iota(jnp.int32, (width, slots), 0) == list_ref[0:1, :]
    table = dot_nt(col_hot.astype(F32).astype(BF16), row_hot.astype(F32).astype(BF16))
    out_ref[rows : rows + EXTRA_ROWS, :] = table.astype(BF16)
    seeds_copy.wait()


def restart_kernel(first, me_ref, seeds_ref, *refs):
    out_ref, counts = refs[-3 if first else -2], refs[-1]
    seed_cols = seeds_ref.shape[0]
    low_col = 0 if first else seed_cols // 2
    span = seed_cols // 2
    tiles = counts.shape[1]
    me = me_ref[0]
    spot = lax.broadcasted_iota(jnp.int32, (tiles, TILE), 0)
    offset = spot // 16
    for place, (z, x) in enumerate(ORDER):
        offset = offset + jnp.where((spot // 2) % 8 == place, 4 * z + 2 * x, 0)
    tile_ids = (me ^ offset) * 2 + spot % 2
    lows = lax.broadcasted_iota(jnp.int32, (TILE, TILE), 0)
    if first:
        pick_ref = refs[-2]
        core, x_pos = me % 2, (me // 2) % 2
        pick_row = lax.broadcasted_iota(jnp.int32, pick_ref.shape, 0)
        pick_col = lax.broadcasted_iota(jnp.int32, pick_ref.shape, 1) // TILE
        sib = pick_col // 4
        wanted = 4 * (x_pos ^ ((pick_col // 2) % 2)) + 2 * (core ^ sib) + pick_col % 2
        pick_ref[...] = (pick_row == wanted).astype(F32).astype(BF16)

    @pl.loop(0, span, unroll=16)
    def _(k):
        row = seeds_ref[pl.ds(low_col + k, 1), :]
        high_hot = (tile_ids == row // TILE).astype(F32).astype(BF16)
        low_hot = (lows == row % TILE).astype(F32).astype(BF16)
        counts[k] = dot_nt(high_hot, low_hot) * float(SEED_SHARE)

    for t in range(tiles):
        out_ref[low_col : low_col + span, t * TILE : (t + 1) * TILE] = counts[:, t, :].astype(BF16)
    if not first:
        return
    rest = out_ref.shape[0] - seed_cols
    first = lax.broadcasted_iota(jnp.int32, (rest, out_ref.shape[1]), 0) == 0
    out_ref[seed_cols:, :] = first.astype(F32).astype(BF16)


def stage_kernel(stage, me_ref, rt_ref, pick_ref, *refs):
    own_names, other_names = OWN_STAGES[stage], OTHER_STAGES[stage]
    count = len(own_names) + len(other_names)
    arrivals, refs = refs[:count], refs[count:]
    if stage > 0:
        refs = refs[4 if stage == len(OWN_STAGES) - 1 else 5 :]
    units, bias, kt_ref, total_ref = refs[:4]
    refs = refs[4:]
    me = me_ref[0]
    z_pos = me // 4
    rows = units.shape[0] // 16
    names = [(0, one) for one in own_names] + [(1, one) for one in other_names]
    for (side, one), ref in zip(names, arrivals):
        place = side * 8 + PLACE[one]
        units[place * rows : (place + 1) * rows] = ref[0:rows]
    if names:
        tables = jnp.concatenate(
            [ref[rows : rows + EXTRA_ROWS, 0:TILE] for ref in arrivals], axis=0
        )
        live = jnp.where(dot_nn(tables, pick_ref[...]) > 0.5, -SLOPE, DEAD)
        for at, (side, (z, x)) in enumerate(names):
            group = (side * 2 + x) * 8
            for xs in range(2):
                lane = PLACE[(z, xs)] * rows
                bias[group : group + 8, lane : lane + rows] = live[
                    at * EXTRA_ROWS : at * EXTRA_ROWS + 8, xs * rows : (xs + 1) * rows
                ]
            if side == 0 and z == 0:
                bias[group : group + 8, 8 * rows : 9 * rows] = live[
                    at * EXTRA_ROWS : at * EXTRA_ROWS + 8, 2 * rows : 3 * rows
                ]
    if stage == 0:
        total_ref[...] = jnp.zeros_like(total_ref)
    tasks = stage_tasks(stage)
    for first, end, spans in tasks:
        lanes = slice(first * rows, end * rows)
        for low, high in spans:
            inner = dot_nt(units[low * rows : high * rows, :], units[lanes, :])
            for tile in range((high - low) * rows // TILE):
                source = low + tile // 2
                z, x = ORDER[source % 8]
                bias_row = (source // 8 * 2 + x) * 8 + 2 * (z_pos ^ z) + tile % 2
                shift = bias[pl.ds(bias_row, 1), lanes]
                value = jnp.exp2(inner[tile * TILE : (tile + 1) * TILE] * SLOPE + shift)
                kt_ref[low * rows + tile * TILE : low * rows + (tile + 1) * TILE, lanes] = value.astype(BF16)
    kept = total_ref.shape[0]
    for first, end, spans in tasks:
        if first == 8:
            continue
        lanes = slice(first * rows, min(end, 8) * rows)
        scores = jnp.concatenate([rt_ref[:, low * rows : high * rows] for low, high in spans], axis=1)
        values = jnp.concatenate([kt_ref[low * rows : high * rows, lanes] for low, high in spans], axis=0)
        total_ref[:, lanes] = total_ref[:, lanes] + dot_nn(scores, values)[0:kept]
    if stage < len(OWN_STAGES) - 1:
        if refs:
            refs[0][...] = jnp.zeros_like(refs[0])
        return
    next_ref, gain_ref = refs
    seed_cols = next_ref.shape[0]
    chunk = 512
    for c in range(next_ref.shape[1] // chunk):
        lanes = slice(c * chunk, (c + 1) * chunk)
        gain = DAMPING / total_ref[seed_cols : seed_cols + 8, lanes]
        gain_ref[:, lanes] = gain
        next_ref[:, lanes] = (
            (1.0 - DAMPING) * rt_ref[0:seed_cols, lanes].astype(F32) + total_ref[0:seed_cols, lanes] * gain[0:1]
        ).astype(BF16)


def padded(ranks):
    return jnp.concatenate([ranks, jnp.zeros_like(ranks)], axis=0)


def half_kernel(kt_ref, mine_ref, out_ref):
    seed_cols, own = mine_ref.shape
    mine = padded(mine_ref[...])
    chunk = 512
    for c in range(own // chunk):
        lanes = slice(c * chunk, (c + 1) * chunk)
        out_ref[:, lanes] = dot_nn(mine, kt_ref[0:own, lanes])[0:seed_cols]


def step_kernel(rt_ref, kt_ref, gain_ref, half_ref, other_ref, mine_ref, sent_ref, ranks):
    seed_cols, rows = mine_ref.shape
    own = half_ref.shape[1]
    other = padded(other_ref[...])
    chunk = 512
    for c in range(own // chunk):
        lanes = slice(c * chunk, (c + 1) * chunk)
        total = half_ref[:, lanes] + dot_nn(other, kt_ref[own:, lanes])[0:seed_cols]
        ranks[0:seed_cols, lanes] = (
            (1.0 - DAMPING) * rt_ref[0:seed_cols, lanes].astype(F32) + total * gain_ref[0:1, lanes]
        ).astype(BF16)
    ranks[seed_cols:, :] = jnp.zeros((ranks.shape[0] - seed_cols, own), BF16)
    sent_ref[...] = dot_nn(ranks[...], kt_ref[0:own, own : own + rows])[0:seed_cols]
    mine_ref[...] = dot_nn(ranks[...], kt_ref[0:own, 0:rows])[0:seed_cols]


def last_kernel(rt_ref, gain_ref, mine_ref, other_ref, out_ref):
    seed_cols, rows = out_ref.shape
    total = mine_ref[...] + other_ref[...]
    out_ref[...] = (1.0 - DAMPING) * rt_ref[0:seed_cols, 0:rows].astype(F32) + total * gain_ref[0:1, 0:rows]


WHOLE = pl.BlockSpec(memory_space=pltpu.VMEM)
SCALARS = pl.BlockSpec(memory_space=pltpu.SMEM)
REMAIN = pl.BlockSpec(memory_space=pl.ANY)


def params():
    return pltpu.CompilerParams(vmem_limit_bytes=20 * 2**20)


def in_hbm(array):
    return pltpu.with_memory_space_constraint(array, pltpu.HBM)


def work(micros):
    return pl.CostEstimate(flops=int(micros * 1000), bytes_accessed=int(micros * 100), transcendentals=0)


def swap(array, mapping):
    pairs = [(device, mapping(device)) for device in range(16)]
    return lax.ppermute(array, ("row", "col"), pairs)


def near(device):
    return device ^ 4


def far(device):
    return device ^ 8


def across(device):
    return device ^ 2


def diagonal(device):
    return device ^ 6


def sibling(device):
    return device ^ 1


def chip_local(embeddings, tile_list, tile_count, seeds):
    row_pos = lax.axis_index("row")
    me = (row_pos * 4 + lax.axis_index("col")).reshape(1)
    rows, width = embeddings.shape
    seed_cols = seeds.shape[0]
    sessions = rows * 16
    own = rows * 8
    slots = tile_list.shape[3]
    block, seeds = pl.pallas_call(
        payload_kernel,
        in_specs=[SCALARS] + [REMAIN] * 3,
        out_specs=[WHOLE] * 2,
        out_shape=[
            pltpu.VMEM((rows + EXTRA_ROWS, width), BF16),
            pltpu.VMEM(seeds.shape, seeds.dtype),
        ],
        scratch_shapes=[
            pltpu.VMEM((rows, width), BF16),
            pltpu.VMEM((2, slots), jnp.int32),
            pltpu.SemaphoreType.DMA((3,)),
        ],
        compiler_params=params(),
        name="payload",
    )(tile_count, in_hbm(embeddings), in_hbm(tile_list.reshape(2, slots)), in_hbm(seeds))
    state_shapes = [
        pltpu.VMEM((sessions, width), BF16),
        pltpu.VMEM((32, own + rows), F32),
        pltpu.VMEM((sessions, own + rows), BF16),
        pltpu.VMEM((seed_cols + 8, own), F32),
    ]
    mark = [jax.ShapeDtypeStruct((8, TILE), F32)]

    def run_stage(stage, rt, arrivals, state, extra, *after):
        first_state = 3 + len(arrivals)
        outs = pl.pallas_call(
            functools.partial(stage_kernel, stage),
            in_specs=[SCALARS] + [WHOLE] * (2 + len(arrivals) + len(state)) + [REMAIN] * len(after),
            out_specs=[WHOLE] * (4 + len(extra)),
            out_shape=state_shapes + extra,
            input_output_aliases={first_state + k: k for k in range(len(state))},
            compiler_params=params(),
            cost_estimate=work(2.5),
            name=f"stage{stage}",
        )(me, rt, pick, *arrivals, *state, *after)
        return outs[:4], outs[4:]

    z1 = swap(block, near)
    z2 = swap(block, far)
    x0 = swap(block, across)
    b00 = swap(block, sibling)
    rt, pick = pl.pallas_call(
        functools.partial(restart_kernel, True),
        in_specs=[SCALARS, WHOLE],
        out_specs=[WHOLE] * 2,
        out_shape=[pltpu.VMEM((2 * seed_cols, sessions), BF16), jax.ShapeDtypeStruct((TILE, 6 * TILE), BF16)],
        scratch_shapes=[pltpu.VMEM((seed_cols // 2, sessions // TILE, TILE), F32)],
        compiler_params=params(),
        cost_estimate=work(1.3),
        name="restart",
    )(me, seeds)

    def more_restart(rt):
        return pl.pallas_call(
            functools.partial(restart_kernel, False),
            in_specs=[SCALARS, WHOLE, WHOLE],
            out_specs=WHOLE,
            out_shape=pltpu.VMEM((2 * seed_cols, sessions), BF16),
            input_output_aliases={2: 0},
            scratch_shapes=[pltpu.VMEM((seed_cols // 2, sessions // TILE, TILE), F32)],
            compiler_params=params(),
            cost_estimate=work(1.3),
            name="restart2",
        )(me, seeds, rt)

    z1, x0, rt = lax.optimization_barrier((z1, x0, rt))
    x1 = swap(z1, across)
    b10 = swap(z1, sibling)
    b01 = swap(x0, sibling)
    rt = more_restart(rt)
    state, (done,) = run_stage(0, rt, [block, z1, x0], [], mark)
    z2, b00, done = lax.optimization_barrier((z2, b00, done))
    z3 = swap(z2, near)
    x2 = swap(z2, across)
    state, (done,) = run_stage(1, rt, [z2, b00], state, mark, done)
    z2, done = lax.optimization_barrier((z2, done))
    x3 = swap(z2, diagonal)
    b20 = swap(z2, sibling)
    b11 = swap(x1, sibling)
    state, (done,) = run_stage(2, rt, [x1, b10, b01], state, mark, done)
    x2, z3, done = lax.optimization_barrier((x2, z3, done))
    b30 = swap(z3, sibling)
    b21 = swap(x2, sibling)
    state, (done,) = run_stage(3, rt, [z3, x2, b20, b11], state, mark, done)
    x3, done = lax.optimization_barrier((x3, done))
    b31 = swap(x3, sibling)
    state, _ = run_stage(4, rt, [x3, b30, b21], state, [], done)
    state, (ranks, gain) = run_stage(
        5,
        rt,
        [b31],
        state,
        [jax.ShapeDtypeStruct((seed_cols, own), BF16), jax.ShapeDtypeStruct((8, own), F32)],
    )
    kt = state[2]
    half = pl.pallas_call(
        half_kernel,
        in_specs=[WHOLE] * 2,
        out_specs=WHOLE,
        out_shape=jax.ShapeDtypeStruct((seed_cols, own), F32),
        compiler_params=params(),
        cost_estimate=work(1.5),
        name="half",
    )(kt, ranks)
    mine, sent = pl.pallas_call(
        step_kernel,
        in_specs=[WHOLE] * 5,
        out_specs=[WHOLE] * 2,
        out_shape=[jax.ShapeDtypeStruct((seed_cols, rows), F32)] * 2,
        scratch_shapes=[pltpu.VMEM((2 * seed_cols, own), BF16)],
        compiler_params=params(),
        cost_estimate=work(1.5),
        name="step",
    )(rt, kt, gain, half, swap(ranks, sibling))
    result = pl.pallas_call(
        last_kernel,
        in_specs=[WHOLE] * 4,
        out_specs=WHOLE,
        out_shape=jax.ShapeDtypeStruct((seed_cols, rows), F32),
        compiler_params=params(),
        cost_estimate=work(0.5),
        name="last",
    )(rt, gain, mine, swap(sent, sibling))
    return result.T


def block_width():
    for option_width in (16, 8, 4, 2):
        return option_width
    return 1


def seed_mass(seed_index, is_valid, length):
    spots = jnp.arange(length, dtype=jnp.int32)

    def one_column(pieces):
        index_row, valid_row = pieces
        hits = (index_row[:, None] == spots[None, :]) & valid_row[:, None]
        return jnp.sum(hits.astype(jnp.float32), axis=0) * float(SEED_SHARE)

    table = lax.map(one_column, (seed_index, is_valid))
    return table.T


def grid_local(embeddings, tile_list, tile_count, seeds):
    n_row = lax.axis_size("row")
    n_col = lax.axis_size("col")
    row_pos = lax.axis_index("row")
    col_pos = lax.axis_index("col")
    slice_rows = embeddings.shape[0]
    grid_rows = slice_rows * n_col
    row_tiles = grid_rows // TILE
    col_tiles = slice_rows * n_row // TILE
    seed_cols = seeds.shape[0]
    unit_rows = normalize(embeddings)
    row_emb = lax.all_gather(unit_rows, "col", axis=0, tiled=True).reshape(row_tiles, TILE, -1)
    col_emb = lax.all_gather(unit_rows, "row", axis=0, tiled=True).reshape(col_tiles, TILE, -1)
    slots = tile_list.shape[3]
    width_b = block_width()
    turn_count = slots // width_b
    row_ids = tile_list[0, 0, 0]
    col_ids = tile_list[0, 0, 1]
    live_mask = (jnp.arange(slots, dtype=jnp.int32) < tile_count[0, 0]).astype(jnp.float32)
    row_blocks = row_ids.reshape(turn_count, width_b)
    col_blocks = col_ids.reshape(turn_count, width_b)
    live_blocks = live_mask.reshape(turn_count, width_b)

    def kernel_turn(degree, pieces):
        row_part, col_part, live_part = pieces
        left_tiles = jnp.take(row_emb, row_part, axis=0)
        right_tiles = jnp.take(col_emb, col_part, axis=0)
        inner_prod = jnp.einsum(
            "bie,bje->bij", left_tiles, right_tiles, preferred_element_type=jnp.float32
        )
        values = jnp.exp(KERNEL_GAIN * (2.0 * inner_prod - 2.0)).astype(jnp.bfloat16)
        row_total = jnp.sum(values.astype(jnp.float32), axis=2)
        degree = degree.at[row_part].add(row_total * live_part[:, None])
        return (degree, values)

    degree_part, kernel = lax.scan(
        kernel_turn,
        jnp.zeros((row_tiles, TILE), jnp.float32),
        (row_blocks, col_blocks, live_blocks),
    )
    degree_part = degree_part.reshape(grid_rows)

    def spread(ranks_col):
        col_ranks = ranks_col.reshape(col_tiles, TILE, seed_cols)

        def rank_turn(running, pieces):
            row_part, col_part, live_part, values = pieces
            right_tiles = jnp.take(col_ranks, col_part, axis=0)
            product = jnp.einsum(
                "bij,bjk->bik", values, right_tiles, preferred_element_type=jnp.float32
            )
            running = running.at[row_part].add(product * live_part[:, None, None])
            return (running, None)

        running, unused = lax.scan(
            rank_turn,
            jnp.zeros((row_tiles, TILE, seed_cols), jnp.float32),
            (row_blocks, col_blocks, live_blocks, kernel),
        )
        return running.reshape(grid_rows, seed_cols)

    own_start = (row_pos * n_col + col_pos) * slice_rows
    own_index = seeds - own_start
    seed_own = seed_mass(own_index, (own_index >= 0) & (own_index < slice_rows), slice_rows)
    degree = lax.psum_scatter(degree_part, "col", scatter_dimension=0, tiled=True)
    opening = lax.all_gather(seed_own.astype(jnp.bfloat16), "row", axis=0, tiled=True)
    partial_rows = spread(opening)
    summed = lax.psum_scatter(partial_rows, "col", scatter_dimension=0, tiled=True)
    rank_rows = (1.0 - DAMPING) * seed_own + DAMPING * summed / degree[:, None]
    for sweep_idx in range(ITERS - 1):
        gathered = lax.all_gather(rank_rows.astype(jnp.bfloat16), "row", axis=0, tiled=True)
        partial_rows = spread(gathered)
        summed = lax.psum_scatter(partial_rows, "col", scatter_dimension=0, tiled=True)
        rank_rows = (1.0 - DAMPING) * seed_own + DAMPING * summed / degree[:, None]
    return rank_rows


def solution(mesh):
    n_row, n_col = mesh.shape["row"], mesh.shape["col"]

    def local(embeddings, tile_list, tile_count, seeds):
        small = n_row == 4 and n_col == 4 and embeddings.shape == (2 * TILE, 2 * TILE)
        if small and seeds.shape == (64, TILE):
            return chip_local(embeddings, tile_list, tile_count, seeds)
        return grid_local(embeddings, tile_list, tile_count, seeds)

    return jax.shard_map(
        local,
        mesh=mesh,
        in_specs=(
            P(("groups", "row", "col"), None),
            P(("groups", "row"), "col", None, None),
            P(("groups", "row"), "col"),
            P("groups", None),
        ),
        out_specs=P(("groups", "row", "col"), None),
        check_vma=False,
    )
```

```python
import functools
import math

import jax
import jax.numpy as jnp
from jax import lax
from jax.experimental import pallas as pl
from jax.experimental.pallas import tpu as pltpu
from jax.sharding import PartitionSpec as P

TILE = 128
ITERS = 3
SEED_SHARE = 32


KERNEL_GAIN = 4.0
DAMPING = 0.85
EPSILON = 1e-06

SLOPE = 2.0 * KERNEL_GAIN * math.log2(math.e)
DEAD = -1e9
MASK_ROWS = 16
EXTRA_ROWS = 16

F32 = jnp.float32
BF16 = jnp.bfloat16


def normalize(rows_in):
    widened = rows_in.astype(F32)
    factor = lax.rsqrt(jnp.mean(widened * widened, axis=-1, keepdims=True) + EPSILON)
    return (widened * factor * widened.shape[-1] ** (-0.5)).astype(BF16)


ORDER = ((0, 0), (0, 1), (1, 1), (1, 0), (2, 0), (2, 1), (3, 0), (3, 1))
PLACE = {block: place for place, block in enumerate(ORDER)}
OWN_STAGES = (
    ((0, 0), (1, 0), (0, 1)),
    ((2, 0),),
    ((1, 1),),
    ((3, 0), (2, 1)),
    ((3, 1),),
    (),
)
OTHER_STAGES = (
    (),
    ((0, 0),),
    ((1, 0), (0, 1)),
    ((2, 0), (1, 1)),
    ((3, 0), (2, 1)),
    ((3, 1),),
)


def runs_of(places):
    found = []
    for place in sorted(places):
        if found and found[-1][1] == place:
            found[-1][1] = place + 1
        else:
            found.append([place, place + 1])
    return found


def stage_tasks(stage):
    here, before = set(), set()
    for at_stage in range(stage + 1):
        before = set(here)
        blocks = [set(sum(names[: at_stage + 1], ())) for names in (OWN_STAGES, OTHER_STAGES)]
        for target in blocks[0]:
            for side in (0, 1):
                for source in blocks[side]:
                    if (target[0], source[1]) in blocks[side]:
                        here.add((PLACE[target], side * 8 + PLACE[source]))
        if (0, 0) in blocks[1]:
            here.update((8, PLACE[source]) for source in blocks[0] if (0, source[1]) in blocks[0])
    wanted = {}
    for target, source in here - before:
        wanted.setdefault(target, set()).add(source)
    tasks = []
    for sources in sorted({tuple(sorted(one)) for one in wanted.values()}):
        for low, high in runs_of([target for target in wanted if tuple(sorted(wanted[target])) == sources]):
            tasks.append((low, high, runs_of(sources)))
    return tasks


def dot_nt(lhs, rhs):
    return lax.dot_general(lhs, rhs, (((1,), (1,)), ((), ())), preferred_element_type=F32)


def dot_nn(lhs, rhs):
    return lax.dot_general(lhs, rhs, (((1,), (0,)), ((), ())), preferred_element_type=F32)


def payload_kernel(count_ref, emb_in, list_in, seeds_in, out_ref, seeds_ref, emb_ref, list_ref, sems):
    rows = emb_ref.shape[0]
    width = emb_ref.shape[1]
    slots = list_ref.shape[1]
    emb_copy = pltpu.make_async_copy(emb_in, emb_ref, sems.at[0])
    list_copy = pltpu.make_async_copy(list_in, list_ref, sems.at[1])
    seeds_copy = pltpu.make_async_copy(seeds_in, seeds_ref, sems.at[2])
    emb_copy.start()
    list_copy.start()
    seeds_copy.start()
    emb_copy.wait()
    list_copy.wait()
    out_ref[0:rows, :] = normalize(emb_ref[...])
    live = lax.broadcasted_iota(jnp.int32, (1, slots), 1) < count_ref[0, 0]
    col_hot = (lax.broadcasted_iota(jnp.int32, (EXTRA_ROWS, slots), 0) == list_ref[1:2, :]) & live
    row_hot = lax.broadcasted_iota(jnp.int32, (width, slots), 0) == list_ref[0:1, :]
    table = dot_nt(col_hot.astype(F32).astype(BF16), row_hot.astype(F32).astype(BF16))
    out_ref[rows : rows + EXTRA_ROWS, :] = table.astype(BF16)
    seeds_copy.wait()


def restart_kernel(first, me_ref, seeds_ref, *refs):
    out_ref, counts = refs[-3 if first else -2], refs[-1]
    seed_cols = seeds_ref.shape[0]
    low_col = 0 if first else seed_cols // 2
    span = seed_cols // 2
    tiles = counts.shape[1]
    me = me_ref[0]
    spot = lax.broadcasted_iota(jnp.int32, (tiles, TILE), 0)
    offset = spot // 16
    for place, (z, x) in enumerate(ORDER):
        offset = offset + jnp.where((spot // 2) % 8 == place, 4 * z + 2 * x, 0)
    tile_ids = (me ^ offset) * 2 + spot % 2
    lows = lax.broadcasted_iota(jnp.int32, (TILE, TILE), 0)
    if first:
        pick_ref = refs[-2]
        core, x_pos = me % 2, (me // 2) % 2
        pick_row = lax.broadcasted_iota(jnp.int32, pick_ref.shape, 0)
        pick_col = lax.broadcasted_iota(jnp.int32, pick_ref.shape, 1) // TILE
        sib = pick_col // 4
        wanted = 4 * (x_pos ^ ((pick_col // 2) % 2)) + 2 * (core ^ sib) + pick_col % 2
        pick_ref[...] = (pick_row == wanted).astype(F32).astype(BF16)

    @pl.loop(0, span, unroll=32)
    def _(k):
        row = seeds_ref[pl.ds(low_col + k, 1), :]
        high_hot = (tile_ids == row // TILE).astype(F32).astype(BF16)
        low_hot = (lows == row % TILE).astype(F32).astype(BF16)
        counts[k] = dot_nt(high_hot, low_hot) * float(SEED_SHARE)

    for t in range(tiles):
        out_ref[low_col : low_col + span, t * TILE : (t + 1) * TILE] = counts[:, t, :].astype(BF16)
    if not first:
        return
    rest = out_ref.shape[0] - seed_cols
    first = lax.broadcasted_iota(jnp.int32, (rest, out_ref.shape[1]), 0) == 0
    out_ref[seed_cols:, :] = first.astype(F32).astype(BF16)


def stage_kernel(stage, me_ref, rt_ref, pick_ref, *refs):
    own_names, other_names = OWN_STAGES[stage], OTHER_STAGES[stage]
    count = len(own_names) + len(other_names)
    arrivals, refs = refs[:count], refs[count:]
    if stage > 0:
        refs = refs[4 if stage == len(OWN_STAGES) - 1 else 5 :]
    units, bias, kt_ref, total_ref = refs[:4]
    refs = refs[4:]
    me = me_ref[0]
    z_pos = me // 4
    rows = units.shape[0] // 16
    names = [(0, one) for one in own_names] + [(1, one) for one in other_names]
    for (side, one), ref in zip(names, arrivals):
        place = side * 8 + PLACE[one]
        units[place * rows : (place + 1) * rows] = ref[0:rows]
    if names:
        tables = jnp.concatenate(
            [ref[rows : rows + EXTRA_ROWS, 0:TILE] for ref in arrivals], axis=0
        )
        live = jnp.where(dot_nn(tables, pick_ref[...]) > 0.5, -SLOPE, DEAD)
        for at, (side, (z, x)) in enumerate(names):
            group = (side * 2 + x) * 8
            for xs in range(2):
                lane = PLACE[(z, xs)] * rows
                bias[group : group + 8, lane : lane + rows] = live[
                    at * EXTRA_ROWS : at * EXTRA_ROWS + 8, xs * rows : (xs + 1) * rows
                ]
            if side == 0 and z == 0:
                bias[group : group + 8, 8 * rows : 9 * rows] = live[
                    at * EXTRA_ROWS : at * EXTRA_ROWS + 8, 2 * rows : 3 * rows
                ]
    if stage == 0:
        total_ref[...] = jnp.zeros_like(total_ref)
    tasks = stage_tasks(stage)
    for first, end, spans in tasks:
        lanes = slice(first * rows, end * rows)
        for low, high in spans:
            inner = dot_nt(units[low * rows : high * rows, :], units[lanes, :])
            for tile in range((high - low) * rows // TILE):
                source = low + tile // 2
                z, x = ORDER[source % 8]
                bias_row = (source // 8 * 2 + x) * 8 + 2 * (z_pos ^ z) + tile % 2
                shift = bias[pl.ds(bias_row, 1), lanes]
                value = jnp.exp2(inner[tile * TILE : (tile + 1) * TILE] * SLOPE + shift)
                kt_ref[low * rows + tile * TILE : low * rows + (tile + 1) * TILE, lanes] = value.astype(BF16)
    kept = total_ref.shape[0]
    for first, end, spans in tasks:
        if first == 8:
            continue
        lanes = slice(first * rows, min(end, 8) * rows)
        scores = jnp.concatenate([rt_ref[:, low * rows : high * rows] for low, high in spans], axis=1)
        values = jnp.concatenate([kt_ref[low * rows : high * rows, lanes] for low, high in spans], axis=0)
        total_ref[:, lanes] = total_ref[:, lanes] + dot_nn(scores, values)[0:kept]
    if stage < len(OWN_STAGES) - 1:
        if refs:
            refs[0][...] = jnp.zeros_like(refs[0])
        return
    next_ref, gain_ref = refs
    seed_cols = next_ref.shape[0]
    chunk = 512
    for c in range(next_ref.shape[1] // chunk):
        lanes = slice(c * chunk, (c + 1) * chunk)
        gain = DAMPING / total_ref[seed_cols : seed_cols + 8, lanes]
        gain_ref[:, lanes] = gain
        next_ref[:, lanes] = (
            (1.0 - DAMPING) * rt_ref[0:seed_cols, lanes].astype(F32) + total_ref[0:seed_cols, lanes] * gain[0:1]
        ).astype(BF16)


def padded(ranks):
    return jnp.concatenate([ranks, jnp.zeros_like(ranks)], axis=0)


def half_kernel(kt_ref, mine_ref, out_ref):
    seed_cols, own = mine_ref.shape
    mine = padded(mine_ref[...])
    chunk = 512
    for c in range(own // chunk):
        lanes = slice(c * chunk, (c + 1) * chunk)
        out_ref[:, lanes] = dot_nn(mine, kt_ref[0:own, lanes])[0:seed_cols]


def step_kernel(rt_ref, kt_ref, gain_ref, half_ref, other_ref, mine_ref, sent_ref, ranks):
    seed_cols, rows = mine_ref.shape
    own = half_ref.shape[1]
    other = padded(other_ref[...])
    chunk = 512
    for c in range(own // chunk):
        lanes = slice(c * chunk, (c + 1) * chunk)
        total = half_ref[:, lanes] + dot_nn(other, kt_ref[own:, lanes])[0:seed_cols]
        ranks[0:seed_cols, lanes] = (
            (1.0 - DAMPING) * rt_ref[0:seed_cols, lanes].astype(F32) + total * gain_ref[0:1, lanes]
        ).astype(BF16)
    ranks[seed_cols:, :] = jnp.zeros((ranks.shape[0] - seed_cols, own), BF16)
    sent_ref[...] = dot_nn(ranks[...], kt_ref[0:own, own : own + rows])[0:seed_cols]
    mine_ref[...] = dot_nn(ranks[...], kt_ref[0:own, 0:rows])[0:seed_cols]


def last_kernel(rt_ref, gain_ref, mine_ref, other_ref, out_ref):
    seed_cols, rows = out_ref.shape
    total = mine_ref[...] + other_ref[...]
    out_ref[...] = (1.0 - DAMPING) * rt_ref[0:seed_cols, 0:rows].astype(F32) + total * gain_ref[0:1, 0:rows]


WHOLE = pl.BlockSpec(memory_space=pltpu.VMEM)
SCALARS = pl.BlockSpec(memory_space=pltpu.SMEM)
REMAIN = pl.BlockSpec(memory_space=pl.ANY)


def params():
    return pltpu.CompilerParams(vmem_limit_bytes=20 * 2**20)


def in_hbm(array):
    return pltpu.with_memory_space_constraint(array, pltpu.HBM)


def work(micros):
    return pl.CostEstimate(flops=int(micros * 1000), bytes_accessed=int(micros * 100), transcendentals=0)


def swap(array, mapping):
    pairs = [(device, mapping(device)) for device in range(16)]
    return lax.ppermute(array, ("row", "col"), pairs)


def near(device):
    return device ^ 4


def far(device):
    return device ^ 8


def across(device):
    return device ^ 2


def diagonal(device):
    return device ^ 6


def sibling(device):
    return device ^ 1


def chip_local(embeddings, tile_list, tile_count, seeds):
    row_pos = lax.axis_index("row")
    me = (row_pos * 4 + lax.axis_index("col")).reshape(1)
    rows, width = embeddings.shape
    seed_cols = seeds.shape[0]
    sessions = rows * 16
    own = rows * 8
    slots = tile_list.shape[3]
    block, seeds = pl.pallas_call(
        payload_kernel,
        in_specs=[SCALARS] + [REMAIN] * 3,
        out_specs=[WHOLE] * 2,
        out_shape=[
            pltpu.VMEM((rows + EXTRA_ROWS, width), BF16),
            pltpu.VMEM(seeds.shape, seeds.dtype),
        ],
        scratch_shapes=[
            pltpu.VMEM((rows, width), BF16),
            pltpu.VMEM((2, slots), jnp.int32),
            pltpu.SemaphoreType.DMA((3,)),
        ],
        compiler_params=params(),
        name="payload",
    )(tile_count, in_hbm(embeddings), in_hbm(tile_list.reshape(2, slots)), in_hbm(seeds))
    state_shapes = [
        pltpu.VMEM((sessions, width), BF16),
        pltpu.VMEM((32, own + rows), F32),
        pltpu.VMEM((sessions, own + rows), BF16),
        pltpu.VMEM((seed_cols + 8, own), F32),
    ]
    mark = [jax.ShapeDtypeStruct((8, TILE), F32)]

    def run_stage(stage, rt, arrivals, state, extra, *after):
        first_state = 3 + len(arrivals)
        outs = pl.pallas_call(
            functools.partial(stage_kernel, stage),
            in_specs=[SCALARS] + [WHOLE] * (2 + len(arrivals) + len(state)) + [REMAIN] * len(after),
            out_specs=[WHOLE] * (4 + len(extra)),
            out_shape=state_shapes + extra,
            input_output_aliases={first_state + k: k for k in range(len(state))},
            compiler_params=params(),
            cost_estimate=work(2.5),
            name=f"stage{stage}",
        )(me, rt, pick, *arrivals, *state, *after)
        return outs[:4], outs[4:]

    z1 = swap(block, near)
    z2 = swap(block, far)
    x0 = swap(block, across)
    b00 = swap(block, sibling)
    rt, pick = pl.pallas_call(
        functools.partial(restart_kernel, True),
        in_specs=[SCALARS, WHOLE],
        out_specs=[WHOLE] * 2,
        out_shape=[pltpu.VMEM((2 * seed_cols, sessions), BF16), jax.ShapeDtypeStruct((TILE, 6 * TILE), BF16)],
        scratch_shapes=[pltpu.VMEM((seed_cols // 2, sessions // TILE, TILE), F32)],
        compiler_params=params(),
        cost_estimate=work(1.3),
        name="restart",
    )(me, seeds)

    def more_restart(rt):
        return pl.pallas_call(
            functools.partial(restart_kernel, False),
            in_specs=[SCALARS, WHOLE, WHOLE],
            out_specs=WHOLE,
            out_shape=pltpu.VMEM((2 * seed_cols, sessions), BF16),
            input_output_aliases={2: 0},
            scratch_shapes=[pltpu.VMEM((seed_cols // 2, sessions // TILE, TILE), F32)],
            compiler_params=params(),
            cost_estimate=work(1.3),
            name="restart2",
        )(me, seeds, rt)

    z1, x0, rt = lax.optimization_barrier((z1, x0, rt))
    x1 = swap(z1, across)
    b10 = swap(z1, sibling)
    b01 = swap(x0, sibling)
    rt = more_restart(rt)
    state, (done,) = run_stage(0, rt, [block, z1, x0], [], mark)
    z2, b00, done = lax.optimization_barrier((z2, b00, done))
    z3 = swap(z2, near)
    x2 = swap(z2, across)
    state, (done,) = run_stage(1, rt, [z2, b00], state, mark, done)
    z2, done = lax.optimization_barrier((z2, done))
    x3 = swap(z2, diagonal)
    b20 = swap(z2, sibling)
    b11 = swap(x1, sibling)
    state, (done,) = run_stage(2, rt, [x1, b10, b01], state, mark, done)
    x2, z3, done = lax.optimization_barrier((x2, z3, done))
    b30 = swap(z3, sibling)
    b21 = swap(x2, sibling)
    state, (done,) = run_stage(3, rt, [z3, x2, b20, b11], state, mark, done)
    x3, done = lax.optimization_barrier((x3, done))
    b31 = swap(x3, sibling)
    state, _ = run_stage(4, rt, [x3, b30, b21], state, [], done)
    state, (ranks, gain) = run_stage(
        5,
        rt,
        [b31],
        state,
        [jax.ShapeDtypeStruct((seed_cols, own), BF16), jax.ShapeDtypeStruct((8, own), F32)],
    )
    kt = state[2]
    half = pl.pallas_call(
        half_kernel,
        in_specs=[WHOLE] * 2,
        out_specs=WHOLE,
        out_shape=jax.ShapeDtypeStruct((seed_cols, own), F32),
        compiler_params=params(),
        cost_estimate=work(1.5),
        name="half",
    )(kt, ranks)
    mine, sent = pl.pallas_call(
        step_kernel,
        in_specs=[WHOLE] * 5,
        out_specs=[WHOLE] * 2,
        out_shape=[jax.ShapeDtypeStruct((seed_cols, rows), F32)] * 2,
        scratch_shapes=[pltpu.VMEM((2 * seed_cols, own), BF16)],
        compiler_params=params(),
        cost_estimate=work(1.5),
        name="step",
    )(rt, kt, gain, half, swap(ranks, sibling))
    result = pl.pallas_call(
        last_kernel,
        in_specs=[WHOLE] * 4,
        out_specs=WHOLE,
        out_shape=jax.ShapeDtypeStruct((seed_cols, rows), F32),
        compiler_params=params(),
        cost_estimate=work(0.5),
        name="last",
    )(rt, gain, mine, swap(sent, sibling))
    return result.T


def block_width():
    for option_width in (16, 8, 4, 2):
        return option_width
    return 1


def seed_mass(seed_index, is_valid, length):
    spots = jnp.arange(length, dtype=jnp.int32)

    def one_column(pieces):
        index_row, valid_row = pieces
        hits = (index_row[:, None] == spots[None, :]) & valid_row[:, None]
        return jnp.sum(hits.astype(jnp.float32), axis=0) * float(SEED_SHARE)

    table = lax.map(one_column, (seed_index, is_valid))
    return table.T


def grid_local(embeddings, tile_list, tile_count, seeds):
    n_row = lax.axis_size("row")
    n_col = lax.axis_size("col")
    row_pos = lax.axis_index("row")
    col_pos = lax.axis_index("col")
    slice_rows = embeddings.shape[0]
    grid_rows = slice_rows * n_col
    row_tiles = grid_rows // TILE
    col_tiles = slice_rows * n_row // TILE
    seed_cols = seeds.shape[0]
    unit_rows = normalize(embeddings)
    row_emb = lax.all_gather(unit_rows, "col", axis=0, tiled=True).reshape(row_tiles, TILE, -1)
    col_emb = lax.all_gather(unit_rows, "row", axis=0, tiled=True).reshape(col_tiles, TILE, -1)
    slots = tile_list.shape[3]
    width_b = block_width()
    turn_count = slots // width_b
    row_ids = tile_list[0, 0, 0]
    col_ids = tile_list[0, 0, 1]
    live_mask = (jnp.arange(slots, dtype=jnp.int32) < tile_count[0, 0]).astype(jnp.float32)
    row_blocks = row_ids.reshape(turn_count, width_b)
    col_blocks = col_ids.reshape(turn_count, width_b)
    live_blocks = live_mask.reshape(turn_count, width_b)

    def kernel_turn(degree, pieces):
        row_part, col_part, live_part = pieces
        left_tiles = jnp.take(row_emb, row_part, axis=0)
        right_tiles = jnp.take(col_emb, col_part, axis=0)
        inner_prod = jnp.einsum(
            "bie,bje->bij", left_tiles, right_tiles, preferred_element_type=jnp.float32
        )
        values = jnp.exp(KERNEL_GAIN * (2.0 * inner_prod - 2.0)).astype(jnp.bfloat16)
        row_total = jnp.sum(values.astype(jnp.float32), axis=2)
        degree = degree.at[row_part].add(row_total * live_part[:, None])
        return (degree, values)

    degree_part, kernel = lax.scan(
        kernel_turn,
        jnp.zeros((row_tiles, TILE), jnp.float32),
        (row_blocks, col_blocks, live_blocks),
    )
    degree_part = degree_part.reshape(grid_rows)

    def spread(ranks_col):
        col_ranks = ranks_col.reshape(col_tiles, TILE, seed_cols)

        def rank_turn(running, pieces):
            row_part, col_part, live_part, values = pieces
            right_tiles = jnp.take(col_ranks, col_part, axis=0)
            product = jnp.einsum(
                "bij,bjk->bik", values, right_tiles, preferred_element_type=jnp.float32
            )
            running = running.at[row_part].add(product * live_part[:, None, None])
            return (running, None)

        running, unused = lax.scan(
            rank_turn,
            jnp.zeros((row_tiles, TILE, seed_cols), jnp.float32),
            (row_blocks, col_blocks, live_blocks, kernel),
        )
        return running.reshape(grid_rows, seed_cols)

    own_start = (row_pos * n_col + col_pos) * slice_rows
    own_index = seeds - own_start
    seed_own = seed_mass(own_index, (own_index >= 0) & (own_index < slice_rows), slice_rows)
    degree = lax.psum_scatter(degree_part, "col", scatter_dimension=0, tiled=True)
    opening = lax.all_gather(seed_own.astype(jnp.bfloat16), "row", axis=0, tiled=True)
    partial_rows = spread(opening)
    summed = lax.psum_scatter(partial_rows, "col", scatter_dimension=0, tiled=True)
    rank_rows = (1.0 - DAMPING) * seed_own + DAMPING * summed / degree[:, None]
    for sweep_idx in range(ITERS - 1):
        gathered = lax.all_gather(rank_rows.astype(jnp.bfloat16), "row", axis=0, tiled=True)
        partial_rows = spread(gathered)
        summed = lax.psum_scatter(partial_rows, "col", scatter_dimension=0, tiled=True)
        rank_rows = (1.0 - DAMPING) * seed_own + DAMPING * summed / degree[:, None]
    return rank_rows


def solution(mesh):
    n_row, n_col = mesh.shape["row"], mesh.shape["col"]

    def local(embeddings, tile_list, tile_count, seeds):
        small = n_row == 4 and n_col == 4 and embeddings.shape == (2 * TILE, 2 * TILE)
        if small and seeds.shape == (64, TILE):
            return chip_local(embeddings, tile_list, tile_count, seeds)
        return grid_local(embeddings, tile_list, tile_count, seeds)

    return jax.shard_map(
        local,
        mesh=mesh,
        in_specs=(
            P(("groups", "row", "col"), None),
            P(("groups", "row"), "col", None, None),
            P(("groups", "row"), "col"),
            P("groups", None),
        ),
        out_specs=P(("groups", "row", "col"), None),
        check_vma=False,
    )
```

```python
import functools
import math

import jax
import jax.numpy as jnp
from jax import lax
from jax.experimental import pallas as pl
from jax.experimental.pallas import tpu as pltpu
from jax.sharding import PartitionSpec as P

TILE = 128
ITERS = 3
SEED_SHARE = 32


KERNEL_GAIN = 4.0
DAMPING = 0.85
EPSILON = 1e-06

SLOPE = 2.0 * KERNEL_GAIN * math.log2(math.e)
DEAD = -1e9
MASK_ROWS = 16
EXTRA_ROWS = 16

F32 = jnp.float32
BF16 = jnp.bfloat16


def normalize(rows_in):
    widened = rows_in.astype(F32)
    factor = lax.rsqrt(jnp.mean(widened * widened, axis=-1, keepdims=True) + EPSILON)
    return (widened * factor * widened.shape[-1] ** (-0.5)).astype(BF16)


ORDER = ((0, 0), (0, 1), (1, 1), (1, 0), (2, 0), (2, 1), (3, 0), (3, 1))
PLACE = {block: place for place, block in enumerate(ORDER)}
OWN_STAGES = (
    ((0, 0), (1, 0), (0, 1)),
    ((2, 0),),
    ((1, 1),),
    ((3, 0), (2, 1)),
    ((3, 1),),
    (),
)
OTHER_STAGES = (
    (),
    ((0, 0),),
    ((1, 0), (0, 1)),
    ((2, 0), (1, 1)),
    ((3, 0), (2, 1)),
    ((3, 1),),
)


def runs_of(places):
    found = []
    for place in sorted(places):
        if found and found[-1][1] == place:
            found[-1][1] = place + 1
        else:
            found.append([place, place + 1])
    return found


def stage_tasks(stage):
    here, before = set(), set()
    for at_stage in range(stage + 1):
        before = set(here)
        blocks = [set(sum(names[: at_stage + 1], ())) for names in (OWN_STAGES, OTHER_STAGES)]
        for target in blocks[0]:
            for side in (0, 1):
                for source in blocks[side]:
                    if (target[0], source[1]) in blocks[side]:
                        here.add((PLACE[target], side * 8 + PLACE[source]))
        if (0, 0) in blocks[1]:
            here.update((8, PLACE[source]) for source in blocks[0] if (0, source[1]) in blocks[0])
    wanted = {}
    for target, source in here - before:
        wanted.setdefault(target, set()).add(source)
    tasks = []
    for sources in sorted({tuple(sorted(one)) for one in wanted.values()}):
        for low, high in runs_of([target for target in wanted if tuple(sorted(wanted[target])) == sources]):
            tasks.append((low, high, runs_of(sources)))
    return tasks


def dot_nt(lhs, rhs):
    return lax.dot_general(lhs, rhs, (((1,), (1,)), ((), ())), preferred_element_type=F32)


def dot_nn(lhs, rhs):
    return lax.dot_general(lhs, rhs, (((1,), (0,)), ((), ())), preferred_element_type=F32)


def payload_kernel(count_ref, emb_in, list_in, seeds_in, out_ref, seeds_ref, emb_ref, list_ref, sems):
    rows = emb_ref.shape[0]
    width = emb_ref.shape[1]
    slots = list_ref.shape[1]
    emb_copy = pltpu.make_async_copy(emb_in, emb_ref, sems.at[0])
    list_copy = pltpu.make_async_copy(list_in, list_ref, sems.at[1])
    seeds_copy = pltpu.make_async_copy(seeds_in, seeds_ref, sems.at[2])
    emb_copy.start()
    list_copy.start()
    seeds_copy.start()
    emb_copy.wait()
    list_copy.wait()
    out_ref[0:rows, :] = normalize(emb_ref[...])
    live = lax.broadcasted_iota(jnp.int32, (1, slots), 1) < count_ref[0, 0]
    col_hot = (lax.broadcasted_iota(jnp.int32, (EXTRA_ROWS, slots), 0) == list_ref[1:2, :]) & live
    row_hot = lax.broadcasted_iota(jnp.int32, (width, slots), 0) == list_ref[0:1, :]
    table = dot_nt(col_hot.astype(F32).astype(BF16), row_hot.astype(F32).astype(BF16))
    out_ref[rows : rows + EXTRA_ROWS, :] = table.astype(BF16)
    seeds_copy.wait()


def restart_kernel(first, me_ref, seeds_ref, *refs):
    out_ref, counts = refs[-3 if first else -2], refs[-1]
    seed_cols = seeds_ref.shape[0]
    low_col = 0 if first else seed_cols // 2
    span = seed_cols // 2
    tiles = counts.shape[1]
    me = me_ref[0]
    spot = lax.broadcasted_iota(jnp.int32, (tiles, TILE), 0)
    offset = spot // 16
    for place, (z, x) in enumerate(ORDER):
        offset = offset + jnp.where((spot // 2) % 8 == place, 4 * z + 2 * x, 0)
    tile_ids = (me ^ offset) * 2 + spot % 2
    lows = lax.broadcasted_iota(jnp.int32, (TILE, TILE), 0)
    if first:
        pick_ref = refs[-2]
        core, x_pos = me % 2, (me // 2) % 2
        pick_row = lax.broadcasted_iota(jnp.int32, pick_ref.shape, 0)
        pick_col = lax.broadcasted_iota(jnp.int32, pick_ref.shape, 1) // TILE
        sib = pick_col // 4
        wanted = 4 * (x_pos ^ ((pick_col // 2) % 2)) + 2 * (core ^ sib) + pick_col % 2
        pick_ref[...] = (pick_row == wanted).astype(F32).astype(BF16)

    @pl.loop(0, span, unroll=32)
    def _(k):
        row = seeds_ref[pl.ds(low_col + k, 1), :]
        high_hot = (tile_ids == row // TILE).astype(F32).astype(BF16)
        low_hot = (lows == row % TILE).astype(F32).astype(BF16)
        counts[k] = dot_nt(high_hot, low_hot) * float(SEED_SHARE)

    for t in range(tiles):
        out_ref[low_col : low_col + span, t * TILE : (t + 1) * TILE] = counts[:, t, :].astype(BF16)
    if not first:
        return
    rest = out_ref.shape[0] - seed_cols
    first = lax.broadcasted_iota(jnp.int32, (rest, out_ref.shape[1]), 0) == 0
    out_ref[seed_cols:, :] = first.astype(F32).astype(BF16)


def stage_kernel(stage, me_ref, rt_ref, pick_ref, *refs):
    own_names, other_names = OWN_STAGES[stage], OTHER_STAGES[stage]
    count = len(own_names) + len(other_names)
    arrivals, refs = refs[:count], refs[count:]
    if stage > 0:
        refs = refs[4 if stage == len(OWN_STAGES) - 1 else 5 :]
    units, bias, kt_ref, total_ref = refs[:4]
    refs = refs[4:]
    me = me_ref[0]
    z_pos = me // 4
    rows = units.shape[0] // 16
    names = [(0, one) for one in own_names] + [(1, one) for one in other_names]
    for (side, one), ref in zip(names, arrivals):
        place = side * 8 + PLACE[one]
        units[place * rows : (place + 1) * rows] = ref[0:rows]
    if names:
        tables = jnp.concatenate(
            [ref[rows : rows + EXTRA_ROWS, 0:TILE] for ref in arrivals], axis=0
        )
        live = jnp.where(dot_nn(tables, pick_ref[...]) > 0.5, -SLOPE, DEAD)
        for at, (side, (z, x)) in enumerate(names):
            group = (side * 2 + x) * 8
            for xs in range(2):
                lane = PLACE[(z, xs)] * rows
                bias[group : group + 8, lane : lane + rows] = live[
                    at * EXTRA_ROWS : at * EXTRA_ROWS + 8, xs * rows : (xs + 1) * rows
                ]
            if side == 0 and z == 0:
                bias[group : group + 8, 8 * rows : 9 * rows] = live[
                    at * EXTRA_ROWS : at * EXTRA_ROWS + 8, 2 * rows : 3 * rows
                ]
    if stage == 0:
        total_ref[...] = jnp.zeros_like(total_ref)
    tasks = stage_tasks(stage)
    for first, end, spans in tasks:
        lanes = slice(first * rows, end * rows)
        for low, high in spans:
            inner = dot_nt(units[low * rows : high * rows, :], units[lanes, :])
            for tile in range((high - low) * rows // TILE):
                source = low + tile // 2
                z, x = ORDER[source % 8]
                bias_row = (source // 8 * 2 + x) * 8 + 2 * (z_pos ^ z) + tile % 2
                shift = bias[pl.ds(bias_row, 1), lanes]
                value = jnp.exp2(inner[tile * TILE : (tile + 1) * TILE] * SLOPE + shift)
                kt_ref[low * rows + tile * TILE : low * rows + (tile + 1) * TILE, lanes] = value.astype(BF16)
    kept = total_ref.shape[0]
    for first, end, spans in tasks:
        if first == 8:
            continue
        lanes = slice(first * rows, min(end, 8) * rows)
        scores = jnp.concatenate([rt_ref[:, low * rows : high * rows] for low, high in spans], axis=1)
        values = jnp.concatenate([kt_ref[low * rows : high * rows, lanes] for low, high in spans], axis=0)
        total_ref[:, lanes] = total_ref[:, lanes] + dot_nn(scores, values)[0:kept]
    if stage < len(OWN_STAGES) - 1:
        if refs:
            refs[0][...] = jnp.zeros_like(refs[0])
        return
    next_ref, gain_ref = refs
    seed_cols = next_ref.shape[0]
    chunk = 512
    for c in range(next_ref.shape[1] // chunk):
        lanes = slice(c * chunk, (c + 1) * chunk)
        gain = DAMPING / total_ref[seed_cols : seed_cols + 8, lanes]
        gain_ref[:, lanes] = gain
        next_ref[:, lanes] = (
            (1.0 - DAMPING) * rt_ref[0:seed_cols, lanes].astype(F32) + total_ref[0:seed_cols, lanes] * gain[0:1]
        ).astype(BF16)


def padded(ranks):
    return jnp.concatenate([ranks, jnp.zeros_like(ranks)], axis=0)


def half_kernel(kt_ref, mine_ref, out_ref):
    seed_cols, own = mine_ref.shape
    mine = padded(mine_ref[...])
    chunk = 512
    for c in range(own // chunk):
        lanes = slice(c * chunk, (c + 1) * chunk)
        out_ref[:, lanes] = dot_nn(mine, kt_ref[0:own, lanes])[0:seed_cols]


def step_kernel(rt_ref, kt_ref, gain_ref, half_ref, other_ref, mine_ref, sent_ref, ranks):
    seed_cols, rows = mine_ref.shape
    own = half_ref.shape[1]
    other = padded(other_ref[...])
    chunk = 512
    for c in range(own // chunk):
        lanes = slice(c * chunk, (c + 1) * chunk)
        total = half_ref[:, lanes] + dot_nn(other, kt_ref[own:, lanes])[0:seed_cols]
        ranks[0:seed_cols, lanes] = (
            (1.0 - DAMPING) * rt_ref[0:seed_cols, lanes].astype(F32) + total * gain_ref[0:1, lanes]
        ).astype(BF16)
    ranks[seed_cols:, :] = jnp.zeros((ranks.shape[0] - seed_cols, own), BF16)
    sent_ref[...] = dot_nn(ranks[...], kt_ref[0:own, own : own + rows])[0:seed_cols]
    mine_ref[...] = dot_nn(ranks[...], kt_ref[0:own, 0:rows])[0:seed_cols]


def last_kernel(rt_ref, gain_ref, mine_ref, other_ref, out_ref):
    seed_cols, rows = out_ref.shape
    total = mine_ref[...] + other_ref[...]
    out_ref[...] = (1.0 - DAMPING) * rt_ref[0:seed_cols, 0:rows].astype(F32) + total * gain_ref[0:1, 0:rows]


WHOLE = pl.BlockSpec(memory_space=pltpu.VMEM)
SCALARS = pl.BlockSpec(memory_space=pltpu.SMEM)
REMAIN = pl.BlockSpec(memory_space=pl.ANY)


def params():
    return pltpu.CompilerParams(vmem_limit_bytes=20 * 2**20)


def in_hbm(array):
    return pltpu.with_memory_space_constraint(array, pltpu.HBM)


def work(micros):
    return pl.CostEstimate(flops=int(micros * 1000), bytes_accessed=int(micros * 100), transcendentals=0)


def swap(array, mapping):
    pairs = [(device, mapping(device)) for device in range(16)]
    return lax.ppermute(array, ("row", "col"), pairs)


def near(device):
    return device ^ 4


def far(device):
    return device ^ 8


def across(device):
    return device ^ 2


def diagonal(device):
    return device ^ 6


def sibling(device):
    return device ^ 1


def chip_local(embeddings, tile_list, tile_count, seeds):
    row_pos = lax.axis_index("row")
    me = (row_pos * 4 + lax.axis_index("col")).reshape(1)
    rows, width = embeddings.shape
    seed_cols = seeds.shape[0]
    sessions = rows * 16
    own = rows * 8
    slots = tile_list.shape[3]
    block, seeds = pl.pallas_call(
        payload_kernel,
        in_specs=[SCALARS] + [REMAIN] * 3,
        out_specs=[WHOLE] * 2,
        out_shape=[
            pltpu.VMEM((rows + EXTRA_ROWS, width), BF16),
            pltpu.VMEM(seeds.shape, seeds.dtype),
        ],
        scratch_shapes=[
            pltpu.VMEM((rows, width), BF16),
            pltpu.VMEM((2, slots), jnp.int32),
            pltpu.SemaphoreType.DMA((3,)),
        ],
        compiler_params=params(),
        name="payload",
    )(tile_count, in_hbm(embeddings), in_hbm(tile_list.reshape(2, slots)), in_hbm(seeds))
    state_shapes = [
        pltpu.VMEM((sessions, width), BF16),
        pltpu.VMEM((32, own + rows), F32),
        pltpu.VMEM((sessions, own + rows), BF16),
        pltpu.VMEM((seed_cols + 8, own), F32),
    ]
    mark = [jax.ShapeDtypeStruct((8, TILE), F32)]

    def run_stage(stage, rt, arrivals, state, extra, *after):
        first_state = 3 + len(arrivals)
        outs = pl.pallas_call(
            functools.partial(stage_kernel, stage),
            in_specs=[SCALARS] + [WHOLE] * (2 + len(arrivals) + len(state)) + [REMAIN] * len(after),
            out_specs=[WHOLE] * (4 + len(extra)),
            out_shape=state_shapes + extra,
            input_output_aliases={first_state + k: k for k in range(len(state))},
            compiler_params=params(),
            cost_estimate=work(2.5),
            name=f"stage{stage}",
        )(me, rt, pick, *arrivals, *state, *after)
        return outs[:4], outs[4:]

    z1 = swap(block, near)
    z2 = swap(block, far)
    x0 = swap(block, across)
    b00 = swap(block, sibling)
    rt, pick = pl.pallas_call(
        functools.partial(restart_kernel, True),
        in_specs=[SCALARS, WHOLE],
        out_specs=[WHOLE] * 2,
        out_shape=[pltpu.VMEM((2 * seed_cols, sessions), BF16), jax.ShapeDtypeStruct((TILE, 6 * TILE), BF16)],
        scratch_shapes=[pltpu.VMEM((seed_cols // 2, sessions // TILE, TILE), F32)],
        compiler_params=params(),
        cost_estimate=work(1.3),
        name="restart",
    )(me, seeds)

    def more_restart(rt):
        return pl.pallas_call(
            functools.partial(restart_kernel, False),
            in_specs=[SCALARS, WHOLE, WHOLE],
            out_specs=WHOLE,
            out_shape=pltpu.VMEM((2 * seed_cols, sessions), BF16),
            input_output_aliases={2: 0},
            scratch_shapes=[pltpu.VMEM((seed_cols // 2, sessions // TILE, TILE), F32)],
            compiler_params=params(),
            cost_estimate=work(1.3),
            name="restart2",
        )(me, seeds, rt)

    z1, x0, rt = lax.optimization_barrier((z1, x0, rt))
    x1 = swap(z1, across)
    b10 = swap(z1, sibling)
    b01 = swap(x0, sibling)
    rt = more_restart(rt)
    state, (done,) = run_stage(0, rt, [block, z1, x0], [], mark)
    z2, b00, done = lax.optimization_barrier((z2, b00, done))
    z3 = swap(z2, near)
    x2 = swap(z2, across)
    state, (done,) = run_stage(1, rt, [z2, b00], state, mark, done)
    z2, done = lax.optimization_barrier((z2, done))
    x3 = swap(z2, diagonal)
    b20 = swap(z2, sibling)
    b11 = swap(x1, sibling)
    state, (done,) = run_stage(2, rt, [x1, b10, b01], state, mark, done)
    z3, x2, done = lax.optimization_barrier((z3, x2, done))
    b30 = swap(z3, sibling)
    b21 = swap(x2, sibling)
    state, (done,) = run_stage(3, rt, [z3, x2, b20, b11], state, mark, done)
    x3, done = lax.optimization_barrier((x3, done))
    b31 = swap(x3, sibling)
    state, _ = run_stage(4, rt, [x3, b30, b21], state, [], done)
    state, (ranks, gain) = run_stage(
        5,
        rt,
        [b31],
        state,
        [jax.ShapeDtypeStruct((seed_cols, own), BF16), jax.ShapeDtypeStruct((8, own), F32)],
    )
    kt = state[2]
    half = pl.pallas_call(
        half_kernel,
        in_specs=[WHOLE] * 2,
        out_specs=WHOLE,
        out_shape=jax.ShapeDtypeStruct((seed_cols, own), F32),
        compiler_params=params(),
        cost_estimate=work(1.5),
        name="half",
    )(kt, ranks)
    mine, sent = pl.pallas_call(
        step_kernel,
        in_specs=[WHOLE] * 5,
        out_specs=[WHOLE] * 2,
        out_shape=[jax.ShapeDtypeStruct((seed_cols, rows), F32)] * 2,
        scratch_shapes=[pltpu.VMEM((2 * seed_cols, own), BF16)],
        compiler_params=params(),
        cost_estimate=work(1.5),
        name="step",
    )(rt, kt, gain, half, swap(ranks, sibling))
    result = pl.pallas_call(
        last_kernel,
        in_specs=[WHOLE] * 4,
        out_specs=WHOLE,
        out_shape=jax.ShapeDtypeStruct((seed_cols, rows), F32),
        compiler_params=params(),
        cost_estimate=work(0.5),
        name="last",
    )(rt, gain, mine, swap(sent, sibling))
    return result.T


def block_width():
    for option_width in (16, 8, 4, 2):
        return option_width
    return 1


def seed_mass(seed_index, is_valid, length):
    spots = jnp.arange(length, dtype=jnp.int32)

    def one_column(pieces):
        index_row, valid_row = pieces
        hits = (index_row[:, None] == spots[None, :]) & valid_row[:, None]
        return jnp.sum(hits.astype(jnp.float32), axis=0) * float(SEED_SHARE)

    table = lax.map(one_column, (seed_index, is_valid))
    return table.T


def grid_local(embeddings, tile_list, tile_count, seeds):
    n_row = lax.axis_size("row")
    n_col = lax.axis_size("col")
    row_pos = lax.axis_index("row")
    col_pos = lax.axis_index("col")
    slice_rows = embeddings.shape[0]
    grid_rows = slice_rows * n_col
    row_tiles = grid_rows // TILE
    col_tiles = slice_rows * n_row // TILE
    seed_cols = seeds.shape[0]
    unit_rows = normalize(embeddings)
    row_emb = lax.all_gather(unit_rows, "col", axis=0, tiled=True).reshape(row_tiles, TILE, -1)
    col_emb = lax.all_gather(unit_rows, "row", axis=0, tiled=True).reshape(col_tiles, TILE, -1)
    slots = tile_list.shape[3]
    width_b = block_width()
    turn_count = slots // width_b
    row_ids = tile_list[0, 0, 0]
    col_ids = tile_list[0, 0, 1]
    live_mask = (jnp.arange(slots, dtype=jnp.int32) < tile_count[0, 0]).astype(jnp.float32)
    row_blocks = row_ids.reshape(turn_count, width_b)
    col_blocks = col_ids.reshape(turn_count, width_b)
    live_blocks = live_mask.reshape(turn_count, width_b)

    def kernel_turn(degree, pieces):
        row_part, col_part, live_part = pieces
        left_tiles = jnp.take(row_emb, row_part, axis=0)
        right_tiles = jnp.take(col_emb, col_part, axis=0)
        inner_prod = jnp.einsum(
            "bie,bje->bij", left_tiles, right_tiles, preferred_element_type=jnp.float32
        )
        values = jnp.exp(KERNEL_GAIN * (2.0 * inner_prod - 2.0)).astype(jnp.bfloat16)
        row_total = jnp.sum(values.astype(jnp.float32), axis=2)
        degree = degree.at[row_part].add(row_total * live_part[:, None])
        return (degree, values)

    degree_part, kernel = lax.scan(
        kernel_turn,
        jnp.zeros((row_tiles, TILE), jnp.float32),
        (row_blocks, col_blocks, live_blocks),
    )
    degree_part = degree_part.reshape(grid_rows)

    def spread(ranks_col):
        col_ranks = ranks_col.reshape(col_tiles, TILE, seed_cols)

        def rank_turn(running, pieces):
            row_part, col_part, live_part, values = pieces
            right_tiles = jnp.take(col_ranks, col_part, axis=0)
            product = jnp.einsum(
                "bij,bjk->bik", values, right_tiles, preferred_element_type=jnp.float32
            )
            running = running.at[row_part].add(product * live_part[:, None, None])
            return (running, None)

        running, unused = lax.scan(
            rank_turn,
            jnp.zeros((row_tiles, TILE, seed_cols), jnp.float32),
            (row_blocks, col_blocks, live_blocks, kernel),
        )
        return running.reshape(grid_rows, seed_cols)

    own_start = (row_pos * n_col + col_pos) * slice_rows
    own_index = seeds - own_start
    seed_own = seed_mass(own_index, (own_index >= 0) & (own_index < slice_rows), slice_rows)
    degree = lax.psum_scatter(degree_part, "col", scatter_dimension=0, tiled=True)
    opening = lax.all_gather(seed_own.astype(jnp.bfloat16), "row", axis=0, tiled=True)
    partial_rows = spread(opening)
    summed = lax.psum_scatter(partial_rows, "col", scatter_dimension=0, tiled=True)
    rank_rows = (1.0 - DAMPING) * seed_own + DAMPING * summed / degree[:, None]
    for sweep_idx in range(ITERS - 1):
        gathered = lax.all_gather(rank_rows.astype(jnp.bfloat16), "row", axis=0, tiled=True)
        partial_rows = spread(gathered)
        summed = lax.psum_scatter(partial_rows, "col", scatter_dimension=0, tiled=True)
        rank_rows = (1.0 - DAMPING) * seed_own + DAMPING * summed / degree[:, None]
    return rank_rows


def solution(mesh):
    n_row, n_col = mesh.shape["row"], mesh.shape["col"]

    def local(embeddings, tile_list, tile_count, seeds):
        small = n_row == 4 and n_col == 4 and embeddings.shape == (2 * TILE, 2 * TILE)
        if small and seeds.shape == (64, TILE):
            return chip_local(embeddings, tile_list, tile_count, seeds)
        return grid_local(embeddings, tile_list, tile_count, seeds)

    return jax.shard_map(
        local,
        mesh=mesh,
        in_specs=(
            P(("groups", "row", "col"), None),
            P(("groups", "row"), "col", None, None),
            P(("groups", "row"), "col"),
            P("groups", None),
        ),
        out_specs=P(("groups", "row", "col"), None),
        check_vma=False,
    )
```
